768 devices in a mesh: blk: 48 (over z_hi, y, core), dp: 16 (over x, z_lo).
Axes of the slice: x: 4, y: 8, z: 12 (z_hi: 3, z_lo: 4; z = z_hi * 4 + z_lo), core: 2. Of those that a mesh axis runs over, the one named last changes fastest.
Arguments:
- visual_encodings: bfloat16 [98304, 1152], P(('blk', 'dp')), may hold values from -0.1875 to 0.1875
- sentence_descriptors_prelift: bfloat16 [98304, 1152], P(('blk', 'dp')), may hold values from -0.75 to 0.75
- partner_global_rows: int32 [98304], P(('blk', 'dp')), may hold values from 0 to 98303, as said below
- sentence_lifting_weights: bfloat16 [1152, 1152], replicated, may hold values from -0.1875 to 0.1875
- lifting_perturbation: bfloat16 [1152, 1152], replicated, may hold values from -0.09375 to 0.09375
- logit_scaling_value: float32 [], replicated, may hold values from 2 to 8
- logit_additive_bias: float32 [], replicated, may hold values from -3 to 0
Outputs:
- image_grad: bfloat16 [98304, 1152], P(('blk', 'dp'))
- text_grad: bfloat16 [98304, 1152], P(('blk', 'dp'))
- head_grad: float32 [1152, 576], P('blk', 'dp')
The draws below stay inside these ranges and needn't reach their ends.
Inputs may be any that keep to these rules, and one draw needn't show every extreme that they name: `partner_global_rows`: the text row in block (b, d) names an image row of block ((b + k) mod 48, d) with k 0 or 1.
All inputs are finite; a program needn't handle non-finite values.
Results may differ from the reference program's by a relative error of at most 0.011.
Values may be sent and summed in bfloat16 or wider, within the bound.
A program may use at most 32 MiB of HBM per device.

```python
import math
import jax
import jax.numpy as jnp
from jax import lax

D = 1152
HEAD_COLS = 576
TOK_DEV = 128
TOKENS = 98304
N_BLK = 48
N_DP = 16


def draw_partner_global_rows(key, part):
    key = jax.random.fold_in(key, 7)
    key_ahead, key_within = jax.random.split(key)
    global_rows = jnp.arange(TOKENS, dtype=jnp.int32)
    block_number = global_rows // TOK_DEV
    cycle_place = block_number // N_DP
    data_group = block_number % N_DP
    ahead = jax.random.randint(key_ahead, (TOKENS,), 0, 2, dtype=jnp.int32)
    within = jax.random.randint(key_within, (TOKENS,), 0, TOK_DEV, dtype=jnp.int32)
    first_row = global_rows == 0
    last_row = global_rows == TOKENS - 1
    ahead = jnp.where(first_row | last_row, 0, ahead).astype(jnp.int32)
    within = jnp.where(first_row, 0, jnp.where(last_row, TOK_DEV - 1, within)).astype(jnp.int32)
    target_block = (cycle_place + ahead) % N_BLK * N_DP + data_group
    return (target_block * TOK_DEV + within).astype(jnp.int32)


def strengthened(entries, stream_key, source, target, blocks, factor):
    owner, partner = [(jnp.arange(entries.shape[dim]) // (entries.shape[dim] // blocks)).reshape([-1 if axis == dim else 1 for axis in range(entries.ndim)]) for dim in (source, target)]
    chosen = jax.random.permutation(stream_key, blocks)[partner]
    strong = (owner == chosen) | (owner == (partner + blocks // 2) % blocks)
    return jnp.where(strong, factor * entries, entries)


def block_levels(rng, extent, pieces, smallest, top_value):
    def one(axis_at, shards_of):
        steps = jax.random.uniform(jax.random.fold_in(jax.random.fold_in(rng, 6), axis_at), (shards_of,), jnp.float32, smallest / len(pieces), top_value / len(pieces))
        return jnp.repeat(jnp.exp(steps), extent[axis_at] // shards_of).reshape((-1,) + (1,) * (len(extent) - axis_at - 1))

    level = one(*pieces[0])
    for cut in pieces[1:]:
        level = level * one(*cut)
    return level


def noise(key, dims, width, bound, cuts=(), kind=jnp.bfloat16):
    level = block_levels(key, dims, cuts, -0.22, 0.18) if cuts else 1.0
    values = jax.random.normal(key, dims, jnp.float32) * width * level
    return jnp.minimum(jnp.maximum(values, -bound), bound).astype(kind)


def bell_draw_with(key, dims, deviation, reach, shards, heavy, kind=jnp.bfloat16):
    array = deviation * jax.random.normal(key, dims, jnp.float32)
    if shards:
        array = array * block_levels(key, dims, shards, -0.22, 0.18)
    return jnp.clip(strengthened(array, jax.random.fold_in(key, 3), *heavy), -reach, reach).astype(kind)


def setup_inputs(seed: int = 0) -> dict:
    key_of = jax.random.split(jax.random.key(seed), 8)
    return {
        "visual_encodings": noise(key_of[0], (TOKENS, D), 0.03, 0.1875, ((0, 768),)),
        "sentence_descriptors_prelift": bell_draw_with(key_of[1], (TOKENS, D), 0.03, 0.75, ((0, 768),), (0, 1, 384, 6.0)),
        "partner_global_rows": draw_partner_global_rows(jax.random.fold_in(key_of[7], 71), 0),
        "sentence_lifting_weights": noise(key_of[3], (D, D), D ** -0.5, 0.1875),
        "lifting_perturbation": noise(key_of[4], (D, D), (4 * D) ** -0.5, 0.09375),
        "logit_scaling_value": jnp.clip(jnp.exp(jax.random.uniform(key_of[5], (), jnp.float32, math.log(2.0), math.log(8.0))), 2.0, 8.0),
        "logit_additive_bias": jnp.clip(jax.random.uniform(key_of[6], (), jnp.float32, -3.0, 0.0), -3.0, 0.0),
    }


EPSILON = 1e-06

def sigmoidal_scale_portion(visual_cohort_count, sentence_cohort_count, partner_location_portion, cohort_ordinal, logit_scaling_value, logit_additive_bias):
    angular_closeness_table = logit_scaling_value * jnp.einsum('kgj,koj->kgo', visual_cohort_count.astype(jnp.float32), sentence_cohort_count.astype(jnp.float32)) + logit_additive_bias
    label_sign = jnp.where(partner_location_portion[:, None, :] == cohort_ordinal[:, :, None], 1.0, -1.0).astype(jnp.float32)
    return (-label_sign * jax.nn.sigmoid(-label_sign * angular_closeness_table)).astype(jnp.bfloat16)

def reference(visual_encodings, sentence_descriptors_prelift, partner_global_rows, sentence_lifting_weights, lifting_perturbation, logit_scaling_value, logit_additive_bias):
    perturbed = (sentence_lifting_weights.astype(jnp.float32) + lifting_perturbation.astype(jnp.float32)).astype(jnp.bfloat16)
    projected = jnp.dot(sentence_descriptors_prelift, perturbed, preferred_element_type=jnp.float32)
    text_scale = lax.rsqrt(lax.optimization_barrier(jnp.sum(projected * projected, axis=1, keepdims=True)) + EPSILON)
    caption_unit_length = (projected * text_scale).astype(jnp.bfloat16)
    image_float = visual_encodings.astype(jnp.float32)
    image_scale = lax.rsqrt(lax.optimization_barrier(jnp.sum(image_float * image_float, axis=1, keepdims=True)) + EPSILON)
    visual_direction_vector = (image_float * image_scale).astype(jnp.bfloat16)
    layout = (N_BLK, N_DP, TOK_DEV, D)
    image_blocks = visual_direction_vector.reshape(layout)
    text_blocks = caption_unit_length.reshape(layout)
    pair_blocks = partner_global_rows.reshape(N_BLK, N_DP, TOK_DEV)
    row_blocks = jnp.arange(TOKENS, dtype=jnp.int32).reshape(N_BLK, N_DP, TOK_DEV)
    text_before = jnp.roll(text_blocks, 1, axis=0)
    pair_before = jnp.roll(pair_blocks, 1, axis=0)

    def per_block(inputs):
        visual_cohort_count, present_sentence_rows, former_round_sentence, present_partner_ids, former_round_partner, cohort_ordinal = inputs
        present_coefficient_value = sigmoidal_scale_portion(visual_cohort_count, present_sentence_rows, present_partner_ids, cohort_ordinal, logit_scaling_value, logit_additive_bias).astype(jnp.float32)
        former_round_coefficient = sigmoidal_scale_portion(visual_cohort_count, former_round_sentence, former_round_partner, cohort_ordinal, logit_scaling_value, logit_additive_bias).astype(jnp.float32)
        visual_example = visual_cohort_count.astype(jnp.float32)
        visual_sensitivity = logit_scaling_value * (jnp.einsum('iny,iyt->int', present_coefficient_value, present_sentence_rows.astype(jnp.float32)) + jnp.einsum('iny,iyt->int', former_round_coefficient, former_round_sentence.astype(jnp.float32)))
        present_sensitivity = logit_scaling_value * jnp.einsum('fyl,fyq->flq', present_coefficient_value, visual_example)
        former_round_sensitivity = logit_scaling_value * jnp.einsum('fyl,fyq->flq', former_round_coefficient, visual_example)
        return (visual_sensitivity, present_sensitivity, former_round_sensitivity)
    visual_sensitivity, present_sensitivity, former_round_sensitivity = lax.map(per_block, (image_blocks, text_blocks, text_before, pair_blocks, pair_before, row_blocks))
    visual_direction_sensitivity = visual_sensitivity.reshape(TOKENS, D)
    unit_text_grad = (present_sensitivity + jnp.roll(former_round_sensitivity, -1, axis=0)).reshape(TOKENS, D)
    image_dir = image_float * image_scale
    image_grad = (image_scale * (visual_direction_sensitivity - image_dir * lax.optimization_barrier(jnp.sum(image_dir * visual_direction_sensitivity, axis=1, keepdims=True)))).astype(jnp.bfloat16)
    text_dir = projected * text_scale
    pre_grad = (text_scale * (unit_text_grad - text_dir * lax.optimization_barrier(jnp.sum(text_dir * unit_text_grad, axis=1, keepdims=True)))).astype(jnp.bfloat16)
    text_grad = lax.dot_general(pre_grad, perturbed, (((1,), (1,)), ((), ())), preferred_element_type=jnp.float32).astype(jnp.bfloat16)
    head_grad = lax.dot_general(sentence_descriptors_prelift, pre_grad[:, :HEAD_COLS], (((0,), (0,)), ((), ())), preferred_element_type=jnp.float32)
    return (image_grad, text_grad, head_grad)
```

```python
import functools

import jax
import jax.numpy as jnp
from jax import lax
from jax.experimental import pallas as pl
from jax.experimental.pallas import tpu as pltpu
from jax.sharding import PartitionSpec as P

D = 1152
HEAD_COLS = 576
ROWS = 128
EPSILON = 1e-06
MESH = pl.DeviceIdType.MESH
NX, NY, NZ, NC, ZL = 4, 8, 12, 2, 4
GROUP = NX * NC
W_CHUNKS = 3
WC = D // W_CHUNKS


def device_at(x, y, z, c):
    x, y, z, c = lax.rem(x, NX), lax.rem(y, NY), lax.rem(z, NZ), lax.rem(c, NC)
    return ((z // ZL) * NY + y) * NC + c, x * ZL + lax.rem(z, ZL)


def coefficients(logits, ids, base):
    image_rows = base + lax.broadcasted_iota(jnp.int32, logits.shape, 0)
    match = image_rows == ids
    value = jax.nn.sigmoid(jnp.where(match, -logits, logits))
    return jnp.where(match, -value, value).astype(jnp.bfloat16)


def nt(left, right):
    return lax.dot_general(left, right, (((1,), (1,)), ((), ())), preferred_element_type=jnp.float32)


def tn(left, right):
    return lax.dot_general(left, right, (((0,), (0,)), ((), ())), preferred_element_type=jnp.float32)


def unit_scale(values):
    return lax.rsqrt(jnp.sum(values * values, axis=1, keepdims=True) + EPSILON)


def kernel(
    img_hbm, desc_hbm, ids_hbm, w_hbm, dw_hbm, scale_ref, bias_ref,
    image_grad_hbm, text_grad_hbm, head_ref,
    imgs, img_units, descs, ids, ids_prev, w, dw, pert, proj, text_unit,
    at_send, at_all, pt_send, pt_all, r_buf, y_own, y_send, y_recv, z_send, z_recv,
    image_out, text_out,
    local_sem, out_sem, ring_send, ring_recv, a_send_sem, a_recv_sem, p_send_sem, p_recv_sem,
    y_send_sem, y_recv_sem, z_send_sem, z_recv_sem,
):
    b = lax.axis_index("blk")
    d = lax.axis_index("dp")
    c, y, z, x = lax.rem(b, 2), lax.rem(b // 2, NY), (b // (2 * NY)) * ZL + lax.rem(d, ZL), d // ZL
    after = (lax.rem(b + 1, 48), d)
    before = (lax.rem(b + 47, 48), d)
    group = [(i, f) for i in range(NX) for f in range(NC) if (i, f) != (0, 0)]

    barrier = pltpu.get_barrier_semaphore()
    for i, f in group:
        pl.semaphore_signal(barrier, inc=1, device_id=device_at(x + i, y, z, c + f), device_id_type=MESH)
    across = (lax.rem(b + 47 + 2 * c, 48), d)
    pl.semaphore_signal(barrier, inc=1, device_id=across, device_id_type=MESH)
    for j in range(1, NY):
        pl.semaphore_signal(barrier, inc=1, device_id=device_at(x, y + j, z, c), device_id_type=MESH)
    for j in range(1, NZ):
        pl.semaphore_signal(barrier, inc=1, device_id=device_at(x, y, z + j, c), device_id_type=MESH)

    loads = [
        pltpu.make_async_copy(desc_hbm, descs.at[pl.ds(0, ROWS)], local_sem.at[0]),
        pltpu.make_async_copy(img_hbm, imgs.at[pl.ds(0, ROWS)], local_sem.at[1]),
        pltpu.make_async_copy(ids_hbm, ids, local_sem.at[2]),
    ]
    loads[0].start()
    w_loads = []
    for n in range(W_CHUNKS):
        cols = pl.ds(n * WC, WC)
        pair = [
            pltpu.make_async_copy(w_hbm.at[:, cols], w.at[:, cols], local_sem.at[3 + 2 * n]),
            pltpu.make_async_copy(dw_hbm.at[:, cols], dw.at[:, cols], local_sem.at[4 + 2 * n]),
        ]
        for copy in pair:
            copy.start()
        w_loads.append(pair)
    loads[1].start()
    loads[2].start()

    loads[0].wait()
    desc = descs[pl.ds(0, ROWS), :]
    turned = jnp.transpose(desc.astype(jnp.float32)).reshape(24, 2, 24, ROWS)
    for parity in range(2):
        at_send[parity] = turned[:, parity].reshape(HEAD_COLS, ROWS).astype(jnp.bfloat16)
    loads[1].wait()
    loads[2].wait()

    pl.semaphore_wait(barrier, len(group) + 1 + NY - 1 + NZ - 1)

    def remote(src, dst, send, recv, device):
        return pltpu.make_async_remote_copy(
            src_ref=src, dst_ref=dst, send_sem=send, recv_sem=recv, device_id=device, device_id_type=MESH
        )

    send_img = remote(imgs.at[pl.ds(0, ROWS)], imgs.at[pl.ds(ROWS, ROWS)], ring_send.at[0], ring_recv.at[0], before)
    send_img.start()
    send_desc = remote(descs.at[pl.ds(0, ROWS)], descs.at[pl.ds(ROWS, ROWS)], ring_send.at[1], ring_recv.at[1], after)
    send_ids = remote(ids, ids_prev, ring_send.at[2], ring_recv.at[2], after)
    a_copies = []
    for i, f in group:
        s = i * NC + f
        copy = remote(
            at_send.at[lax.rem(c + f, NC)], at_all.at[:, pl.ds(s * ROWS, ROWS)],
            a_send_sem.at[s], a_recv_sem.at[s], device_at(x + i, y, z, c + f),
        )
        copy.start()
        a_copies.append(copy)
    send_desc.start()
    send_ids.start()

    for n in range(W_CHUNKS):
        cols = pl.ds(n * WC, WC)
        for copy in w_loads[n]:
            copy.wait()
        part = (w[:, cols].astype(jnp.float32) + dw[:, cols].astype(jnp.float32)).astype(jnp.bfloat16)
        pert[:, cols] = part
        proj[:, cols] = jnp.dot(descs[pl.ds(0, ROWS), :], part, preferred_element_type=jnp.float32)
    projected = proj[...]
    text_scale = unit_scale(projected)
    unit = projected * text_scale
    proj[...] = unit
    text_unit[pl.ds(0, ROWS), :] = unit.astype(jnp.bfloat16)

    img = imgs[pl.ds(0, ROWS), :].astype(jnp.float32)
    image_scale = unit_scale(img)
    img_units[pl.ds(0, ROWS), :] = (img * image_scale).astype(jnp.bfloat16)
    at_all[:, pl.ds(0, ROWS)] = at_send[c]

    scale = scale_ref[0]
    bias = bias_ref[0]
    row_base = (b * 16 + d) * ROWS
    next_base = (after[0] * 16 + d) * ROWS

    send_img.wait_recv()
    img_next = imgs[pl.ds(ROWS, ROWS), :].astype(jnp.float32)
    img_units[pl.ds(ROWS, ROWS), :] = (img_next * unit_scale(img_next)).astype(jnp.bfloat16)
    logits = scale * nt(img_units[...], text_unit[pl.ds(0, ROWS), :]) + bias
    my_ids = ids[...]
    coef_own = coefficients(logits[:ROWS], my_ids, row_base)
    coef_next = coefficients(logits[ROWS:], my_ids, next_base)
    unit_text_grad = scale * tn(jnp.concatenate([coef_own, coef_next], axis=0), img_units[...])
    along = jnp.sum(unit * unit_text_grad, axis=1, keepdims=True)
    pre_grad = text_scale * (unit_text_grad - unit * along)
    pt = jnp.transpose(pre_grad[:, :HEAD_COLS])
    pt_send[...] = pt.reshape(NX, HEAD_COLS // NX, ROWS).astype(jnp.bfloat16)
    p_copies = []
    for i, f in group:
        s = i * NC + f
        copy = remote(
            pt_send.at[lax.rem(x + i, NX)], pt_all.at[:, pl.ds(s * ROWS, ROWS)],
            p_send_sem.at[s], p_recv_sem.at[s], device_at(x + i, y, z, c + f),
        )
        copy.start()
        p_copies.append(copy)
    pt_all[:, pl.ds(0, ROWS)] = pt_send[x]

    text_out[...] = nt(pre_grad.astype(jnp.bfloat16), pert[...]).astype(jnp.bfloat16)
    text_copy = pltpu.make_async_copy(text_out, text_grad_hbm, out_sem.at[0])
    text_copy.start()

    for copy in a_copies:
        copy.wait_recv()
    for copy in p_copies:
        copy.wait_recv()
    r_buf[:, pl.ds(0, 144)] = nt(at_all[...], pt_all[...])
    low = r_buf[:, pl.ds(0, 128)].reshape(24, 3, 8, 128)
    high = r_buf[:, pl.ds(128, 128)].reshape(24, 3, 8, 128)
    lane = lax.broadcasted_iota(jnp.int32, (24, 8, 128), 2)

    def moved(values, shift):
        shift = shift % 128
        return pltpu.roll(values, shift, 2) if shift else values

    for k in range(ZL):
        parts = []
        for o in range(3):
            part = moved(low[:, o], 36 * o - 36 * k)
            if k == ZL - 1:
                part = jnp.where(lane < 36 * o + 20, part, moved(high[:, o], 36 * o + 20))
            parts.append(part)
        tile = jnp.where(lane < 36, parts[0], jnp.where(lane < 72, parts[1], parts[2]))
        tile = jnp.where(lane < 108, tile, 0.0).reshape(3, NY, 8, 128)
        for h in range(3):
            y_own[:, pl.ds((h * ZL + k) * 8, 8), :] = tile[h]
    y_send[...] = y_own[...].astype(jnp.bfloat16)
    y_copies = []
    for j in range(1, NY):
        copy = remote(
            y_send.at[lax.rem(y + j, NY)], y_recv.at[j], y_send_sem.at[j], y_recv_sem.at[j], device_at(x, y + j, z, c)
        )
        copy.start()
        y_copies.append(copy)

    send_desc.wait_recv()
    send_ids.wait_recv()
    projected_prev = jnp.dot(descs[pl.ds(ROWS, ROWS), :], pert[...], preferred_element_type=jnp.float32)
    text_unit[pl.ds(ROWS, ROWS), :] = (projected_prev * unit_scale(projected_prev)).astype(jnp.bfloat16)
    logits_prev = scale * nt(img_units[pl.ds(0, ROWS), :], text_unit[pl.ds(ROWS, ROWS), :]) + bias
    coef_prev = coefficients(logits_prev, ids_prev[...], row_base)
    unit_image_grad = scale * jnp.dot(
        jnp.concatenate([coef_own, coef_prev], axis=1), text_unit[...], preferred_element_type=jnp.float32
    )
    img = imgs[pl.ds(0, ROWS), :].astype(jnp.float32)
    image_dir = img * image_scale
    along_image = jnp.sum(image_dir * unit_image_grad, axis=1, keepdims=True)
    image_out[...] = (image_scale * (unit_image_grad - image_dir * along_image)).astype(jnp.bfloat16)
    image_copy = pltpu.make_async_copy(image_out, image_grad_hbm, out_sem.at[1])
    image_copy.start()

    total = y_own[y]
    for j, copy in zip(range(1, NY), y_copies):
        copy.wait_recv()
        total = total + y_recv[j].astype(jnp.float32)
    z_send[...] = total.reshape(NZ, 8, 128)
    z_copies = []
    for j in range(1, NZ):
        copy = remote(
            z_send.at[lax.rem(z + j, NZ)], z_recv.at[j], z_send_sem.at[j], z_recv_sem.at[j], device_at(x, y, z + j, c)
        )
        copy.start()
        z_copies.append(copy)
    block = z_send[z]
    for j, copy in zip(range(1, NZ), z_copies):
        copy.wait_recv()
        block = block + z_recv[j]
    for o in range(3):
        head_ref[pl.ds(8 * o, 8), :] = (pltpu.roll(block, 128 - 36 * o, 1) if o else block)[:, :36]

    for copy in [send_img, send_desc, send_ids, *a_copies, *p_copies, *y_copies, *z_copies]:
        copy.wait_send()
    text_copy.wait()
    image_copy.wait()


def shards(img, desc, ids, w, dw, scale, bias):
    bf16, f32 = jnp.bfloat16, jnp.float32
    any_spec = pl.BlockSpec(memory_space=pl.ANY)
    smem = pl.BlockSpec(memory_space=pltpu.SMEM)
    dma = pltpu.SemaphoreType.DMA
    return pl.pallas_call(
        kernel,
        out_shape=(
            jax.ShapeDtypeStruct((ROWS, D), bf16),
            jax.ShapeDtypeStruct((ROWS, D), bf16),
            jax.ShapeDtypeStruct((24, 36), f32),
        ),
        in_specs=[any_spec] * 5 + [smem] * 2,
        out_specs=(any_spec, any_spec, pl.BlockSpec(memory_space=pltpu.VMEM)),
        scratch_shapes=[
            pltpu.VMEM((2 * ROWS, D), bf16),
            pltpu.VMEM((2 * ROWS, D), bf16),
            pltpu.VMEM((2 * ROWS, D), bf16),
            pltpu.VMEM((1, ROWS), jnp.int32),
            pltpu.VMEM((1, ROWS), jnp.int32),
            pltpu.VMEM((D, D), bf16),
            pltpu.VMEM((D, D), bf16),
            pltpu.VMEM((D, D), bf16),
            pltpu.VMEM((ROWS, D), f32),
            pltpu.VMEM((2 * ROWS, D), bf16),
            pltpu.VMEM((2, HEAD_COLS, ROWS), bf16),
            pltpu.VMEM((HEAD_COLS, GROUP * ROWS), bf16),
            pltpu.VMEM((NX, HEAD_COLS // NX, ROWS), bf16),
            pltpu.VMEM((HEAD_COLS // NX, GROUP * ROWS), bf16),
            pltpu.VMEM((HEAD_COLS, 256), f32),
            pltpu.VMEM((NY, 96, 128), f32),
            pltpu.VMEM((NY, 96, 128), bf16),
            pltpu.VMEM((NY, 96, 128), bf16),
            pltpu.VMEM((NZ, 8, 128), f32),
            pltpu.VMEM((NZ, 8, 128), f32),
            pltpu.VMEM((ROWS, D), bf16),
            pltpu.VMEM((ROWS, D), bf16),
            dma((3 + 2 * W_CHUNKS,)),
            dma((2,)),
            dma((3,)),
            dma((3,)),
            dma((GROUP,)),
            dma((GROUP,)),
            dma((GROUP,)),
            dma((GROUP,)),
            dma((NY,)),
            dma((NY,)),
            dma((NZ,)),
            dma((NZ,)),
        ],
        compiler_params=pltpu.CompilerParams(
            collective_id=0, has_side_effects=True, vmem_limit_bytes=63 << 20
        ),
        name="contrastive",
    )(img, desc, ids.reshape(1, ROWS), w, dw, scale.reshape(1), bias.reshape(1))


def solution(mesh):
    rows = P(("blk", "dp"), None)
    return jax.shard_map(
        shards,
        mesh=mesh,
        in_specs=(rows, rows, P(("blk", "dp")), P(), P(), P(), P()),
        out_specs=(rows, rows, P("blk", "dp")),
        check_vma=False,
    )
```

```python
import functools

import jax
import jax.numpy as jnp
from jax import lax
from jax.experimental import pallas as pl
from jax.experimental.pallas import tpu as pltpu
from jax.sharding import PartitionSpec as P

D = 1152
HEAD_COLS = 576
ROWS = 128
EPSILON = 1e-06
MESH = pl.DeviceIdType.MESH
NX, NY, NZ, NC, ZL = 4, 8, 12, 2, 4
GROUP = NX * NC
W_CHUNKS = 3
PLACE_PARTS = 4
IMG_PARTS = ((0, 64), (64, 32), (96, 32))
Y_ORDER = (4, 3, 5, 2, 6, 1, 7)
Z_ORDER = (6, 5, 7, 4, 8, 3, 9, 2, 10, 1, 11)
WC = D // W_CHUNKS


def device_at(x, y, z, c):
    x, y, z, c = lax.rem(x, NX), lax.rem(y, NY), lax.rem(z, NZ), lax.rem(c, NC)
    return ((z // ZL) * NY + y) * NC + c, x * ZL + lax.rem(z, ZL)


def coefficients(logits, ids, base):
    image_rows = base + lax.broadcasted_iota(jnp.int32, logits.shape, 0)
    match = image_rows == ids
    value = jax.nn.sigmoid(jnp.where(match, -logits, logits))
    return jnp.where(match, -value, value).astype(jnp.bfloat16)


def nt(left, right):
    return lax.dot_general(left, right, (((1,), (1,)), ((), ())), preferred_element_type=jnp.float32)


def tn(left, right):
    return lax.dot_general(left, right, (((0,), (0,)), ((), ())), preferred_element_type=jnp.float32)


def unit_scale(values):
    return lax.rsqrt(jnp.sum(values * values, axis=1, keepdims=True) + EPSILON)


def kernel(
    img_hbm, desc_hbm, ids_hbm, w_hbm, dw_hbm, scale_ref, bias_ref,
    image_grad_hbm, text_grad_hbm, head_ref,
    imgs, img_units, descs, ids, ids_prev, w, dw, pert, proj, text_unit,
    at_send, at_all, pt_send, pt_all, r_buf, y_own, y_send, y_recv, z_send, z_recv,
    image_out, text_out,
    local_sem, out_sem, ring_send, ring_recv, a_send_sem, a_recv_sem, p_send_sem, p_recv_sem,
    y_send_sem, y_recv_sem, z_send_sem, z_recv_sem, word, ready, carried, help_recv, carry_send,
):
    b = lax.axis_index("blk")
    d = lax.axis_index("dp")
    c, y, z, x = lax.rem(b, 2), lax.rem(b // 2, NY), (b // (2 * NY)) * ZL + lax.rem(d, ZL), d // ZL
    after = (lax.rem(b + 1, 48), d)
    before = (lax.rem(b + 47, 48), d)
    group = [(i, f) for i in range(NX) for f in range(NC) if (i, f) != (0, 0)]

    barrier = pltpu.get_barrier_semaphore()
    for i, f in group:
        pl.semaphore_signal(barrier, inc=1, device_id=device_at(x + i, y, z, c + f), device_id_type=MESH)
    across = (lax.rem(b + 47 + 2 * c, 48), d)
    goes_out = jnp.logical_and(y == 0, c == 0)
    comes_in = jnp.logical_and(y == NY - 1, c == 1)
    helps = jnp.logical_and(jnp.logical_or(y == NY - 1, y == 1), c == 0)
    helpers = [device_at(x, NY - 1, z + ZL, 0), device_at(x, 1, z + ZL, 0)]

    @pl.when(jnp.logical_not(goes_out))
    def _():
        pl.semaphore_signal(barrier, inc=1, device_id=across, device_id_type=MESH)

    @pl.when(comes_in)
    def _():
        for helper in helpers:
            pl.semaphore_signal(barrier, inc=1, device_id=helper, device_id_type=MESH)

    for j in (1, NY - 1):
        pl.semaphore_signal(barrier, inc=1, device_id=device_at(x, y + j, z, c), device_id_type=MESH)
    for j in (1, NZ - 1):
        pl.semaphore_signal(barrier, inc=1, device_id=device_at(x, y, z + j, c), device_id_type=MESH)

    loads = [
        pltpu.make_async_copy(desc_hbm, descs.at[pl.ds(0, ROWS)], local_sem.at[0]),
        pltpu.make_async_copy(img_hbm, imgs.at[pl.ds(0, ROWS)], local_sem.at[1]),
        pltpu.make_async_copy(ids_hbm, ids, local_sem.at[2]),
    ]
    for copy in loads:
        copy.start()
    w_loads = []
    for n in range(W_CHUNKS):
        cols = pl.ds(n * WC, WC)
        pair = [
            pltpu.make_async_copy(w_hbm.at[:, cols], w.at[:, cols], local_sem.at[3 + 2 * n]),
            pltpu.make_async_copy(dw_hbm.at[:, cols], dw.at[:, cols], local_sem.at[4 + 2 * n]),
        ]
        for copy in pair:
            copy.start()
        w_loads.append(pair)

    loads[0].wait()
    desc = descs[pl.ds(0, ROWS), :]
    turned = jnp.transpose(desc.astype(jnp.float32)).reshape(24, 2, 24, ROWS)
    for parity in range(2):
        at_send[parity] = turned[:, parity].reshape(HEAD_COLS, ROWS).astype(jnp.bfloat16)
    for copy in loads[1:]:
        copy.wait()

    pl.semaphore_wait(barrier, len(group) + 4 + jnp.where(comes_in, 0, 1) + jnp.where(helps, 1, 0))

    def pass_on(round_, along_y, along_z):
        for j in along_y:
            pl.semaphore_signal(
                word.at[2 * round_], inc=1, device_id=device_at(x, y + j, z, c), device_id_type=MESH
            )
        for j in along_z:
            pl.semaphore_signal(
                word.at[2 * round_ + 1], inc=1, device_id=device_at(x, y, z + j, c), device_id_type=MESH
            )

    pass_on(0, (1, NY - 1), (1, NZ - 1))

    def remote(src, dst, send, recv, device):
        return pltpu.make_async_remote_copy(
            src_ref=src, dst_ref=dst, send_sem=send, recv_sem=recv, device_id=device, device_id_type=MESH
        )

    def img_part(part, device):
        rows, n = IMG_PARTS[part]
        return remote(
            imgs.at[pl.ds(rows, n)], imgs.at[pl.ds(ROWS + rows, n)], ring_send.at[part], ring_recv.at[part], device
        )

    def help_part(part, device):
        rows, n = IMG_PARTS[part]
        return remote(imgs.at[pl.ds(rows, n)], carried, ring_send.at[part], help_recv, device)

    send_img = [img_part(part, before) for part in range(3)]

    @pl.when(goes_out)
    def _():
        pl.semaphore_signal(ready, inc=1, device_id=across, device_id_type=MESH)
        help_part(1, device_at(x, NY - 1, z, 0)).start()
        help_part(2, device_at(x, 1, z, 0)).start()
        send_img[0].start()

    @pl.when(jnp.logical_not(goes_out))
    def _():
        for copy in send_img:
            copy.start()

    def slot(i, core):
        return i * NC + core

    first = jnp.where(c == 0, NX - 1, 1)
    a_copies = []
    for n, (i, f) in enumerate([(first, 0), (first, 1), (0, 1), (NX - first, 0), (NX - first, 1)]):
        copy = remote(
            at_send.at[lax.rem(c + f, NC)], at_all.at[slot(i, c)],
            a_send_sem.at[n], a_recv_sem.at[slot(i, c)], device_at(x + i, y, z, c + f),
        )
        copy.start()
        a_copies.append(copy)

    def a_arrived(s):
        return remote(at_send.at[0], at_all.at[s], a_send_sem.at[0], a_recv_sem.at[s], before)

    def p_arrived(s):
        return remote(pt_send.at[0], pt_all.at[s], p_send_sem.at[0], p_recv_sem.at[s], before)

    for n in range(W_CHUNKS):
        cols = pl.ds(n * WC, WC)
        for copy in w_loads[n]:
            copy.wait()
        part = (w[:, cols].astype(jnp.float32) + dw[:, cols].astype(jnp.float32)).astype(jnp.bfloat16)
        pert[:, cols] = part
        proj[:, cols] = jnp.dot(descs[pl.ds(0, ROWS), :], part, preferred_element_type=jnp.float32)
    pl.semaphore_wait(word.at[0], 2)
    pl.semaphore_wait(word.at[1], 2)
    pass_on(1, (2, NY - 2), (2, NZ - 2))

    projected = proj[...]
    text_scale = unit_scale(projected)
    unit = projected * text_scale
    proj[...] = unit
    text_unit[pl.ds(0, ROWS), :] = unit.astype(jnp.bfloat16)

    img = imgs[pl.ds(0, ROWS), :].astype(jnp.float32)
    image_scale = unit_scale(img)
    img_units[pl.ds(0, ROWS), :] = (img * image_scale).astype(jnp.bfloat16)
    at_all[slot(0, c)] = at_send[c]

    carry = remote(
        carried,
        imgs.at[pl.ds(ROWS + IMG_PARTS[1][0] + jnp.where(y == 1, IMG_PARTS[1][1], 0), IMG_PARTS[1][1])],
        carry_send, ring_recv.at[jnp.where(y == 1, 2, 1)], device_at(x, NY - 1, z + NZ - ZL, 1),
    )

    @pl.when(helps)
    def _():
        help_part(1, before).wait_recv()
        carry.start()

    @pl.when(comes_in)
    def _():
        pl.semaphore_wait(ready, 1)

    send_desc = remote(descs.at[pl.ds(0, ROWS)], descs.at[pl.ds(ROWS, ROWS)], ring_send.at[3], ring_recv.at[3], after)
    send_ids = remote(ids, ids_prev, ring_send.at[4], ring_recv.at[4], after)
    send_desc.start()
    send_ids.start()

    handed = []
    for n, (i, core) in enumerate([(NX - 1, 0), (1, 1)]):
        a_arrived(slot(i, core)).wait_recv()
        copy = remote(
            at_all.at[slot(i, core)], at_all.at[slot(2, core)],
            a_send_sem.at[5 + n], a_recv_sem.at[slot(2, core)], device_at(x + i, y, z, c),
        )
        copy.start()
        handed.append(copy)

    scale = scale_ref[...]
    bias = bias_ref[...]
    row_base = (b * 16 + d) * ROWS
    next_base = (after[0] * 16 + d) * ROWS

    for copy in send_img:
        copy.wait_recv()
    img_next = imgs[pl.ds(ROWS, ROWS), :].astype(jnp.float32)
    img_units[pl.ds(ROWS, ROWS), :] = (img_next * unit_scale(img_next)).astype(jnp.bfloat16)
    logits = scale * nt(img_units[...], text_unit[pl.ds(0, ROWS), :]) + bias
    my_ids = ids[...]
    coef_own = coefficients(logits[:ROWS], my_ids, row_base)
    coef_next = coefficients(logits[ROWS:], my_ids, next_base)
    unit_text_grad = scale * tn(jnp.concatenate([coef_own, coef_next], axis=0), img_units[...])
    along = jnp.sum(unit * unit_text_grad, axis=1, keepdims=True)
    pre_grad = text_scale * (unit_text_grad - unit * along)
    pt = jnp.transpose(pre_grad[:, :HEAD_COLS])
    pt_send[...] = pt.reshape(NX, HEAD_COLS // NX, ROWS).astype(jnp.bfloat16)
    p_copies = []
    for n, (i, f) in enumerate([(2, 0), (2, 1), (1, 0), (1, 1), (3, 0), (3, 1), (0, 1)]):
        copy = remote(
            pt_send.at[lax.rem(x + i, NX)], pt_all.at[slot(i, c)],
            p_send_sem.at[n], p_recv_sem.at[slot(i, c)], device_at(x + i, y, z, c + f),
        )
        copy.start()
        p_copies.append(copy)
    pt_all[slot(0, c)] = pt_send[x]

    pl.semaphore_wait(word.at[2], 2)
    pl.semaphore_wait(word.at[3], 2)
    pass_on(2, (), (2, NZ - 2))

    text_out[...] = nt(pre_grad.astype(jnp.bfloat16), pert[...]).astype(jnp.bfloat16)
    text_copy = pltpu.make_async_copy(text_out, text_grad_hbm, out_sem.at[0])
    text_copy.start()

    for i in range(NX):
        for core in range(NC):
            if i in (1, 2, 3) and (i, core) not in ((NX - 1, 0), (1, 1)):
                a_arrived(slot(i, core)).wait_recv()
            if i:
                p_arrived(slot(i, core)).wait_recv()
    a_arrived(slot(0, 1 - c)).wait_recv()
    p_arrived(slot(0, 1 - c)).wait_recv()
    features = jnp.concatenate([at_all[s] for s in range(GROUP)], axis=1)
    columns = jnp.concatenate([pt_all[s] for s in range(GROUP)], axis=1)
    r_buf[:, pl.ds(0, 144)] = nt(features, columns)
    low = r_buf[:, pl.ds(0, 128)].reshape(24, 3, 8, 128)
    high = r_buf[:, pl.ds(128, 128)].reshape(24, 3, 8, 128)
    lane = lax.broadcasted_iota(jnp.int32, (24, 8, 128), 2)

    def moved(values, shift):
        shift = shift % 128
        return pltpu.roll(values, shift, 2) if shift else values

    for k in range(ZL):
        parts = []
        for o in range(3):
            part = moved(low[:, o], 36 * o - 36 * k)
            if k == ZL - 1:
                part = jnp.where(lane < 36 * o + 20, part, moved(high[:, o], 36 * o + 20))
            parts.append(part)
        tile = jnp.where(lane < 36, parts[0], jnp.where(lane < 72, parts[1], parts[2]))
        tile = jnp.where(lane < 108, tile, 0.0).reshape(3, NY, 8, 128)
        for h in range(3):
            y_own[:, pl.ds((h * ZL + k) * 8, 8), :] = tile[h]
    y_send[...] = y_own[...].astype(jnp.bfloat16)
    y_copies = []
    for j in Y_ORDER:
        copy = remote(
            y_send.at[lax.rem(y + j, NY)], y_recv.at[j], y_send_sem.at[j], y_recv_sem.at[j], device_at(x, y + j, z, c)
        )
        copy.start()
        y_copies.append(copy)

    total = y_own[y]
    for j, copy in sorted(zip(Y_ORDER, y_copies), key=lambda e: min(e[0], NY - e[0])):
        copy.wait_recv()
        total = total + y_recv[j].astype(jnp.float32)
    pl.semaphore_wait(word.at[5], 2)
    z_send[...] = total.reshape(NZ, 8, 128)
    z_copies = []
    for j in Z_ORDER:
        copy = remote(
            z_send.at[lax.rem(z + j, NZ)], z_recv.at[j], z_send_sem.at[j], z_recv_sem.at[j], device_at(x, y, z + j, c)
        )
        copy.start()
        z_copies.append(copy)
    send_desc.wait_recv()
    send_ids.wait_recv()
    projected_prev = jnp.dot(descs[pl.ds(ROWS, ROWS), :], pert[...], preferred_element_type=jnp.float32)
    text_unit[pl.ds(ROWS, ROWS), :] = (projected_prev * unit_scale(projected_prev)).astype(jnp.bfloat16)
    logits_prev = scale * nt(img_units[pl.ds(0, ROWS), :], text_unit[pl.ds(ROWS, ROWS), :]) + bias
    coef_prev = coefficients(logits_prev, ids_prev[...], row_base)
    unit_image_grad = scale * jnp.dot(
        jnp.concatenate([coef_own, coef_prev], axis=1), text_unit[...], preferred_element_type=jnp.float32
    )
    img = imgs[pl.ds(0, ROWS), :].astype(jnp.float32)
    image_dir = img * image_scale
    along_image = jnp.sum(image_dir * unit_image_grad, axis=1, keepdims=True)
    image_out[...] = (image_scale * (unit_image_grad - image_dir * along_image)).astype(jnp.bfloat16)
    image_copy = pltpu.make_async_copy(image_out, image_grad_hbm, out_sem.at[1])
    image_copy.start()

    block = z_send[z]
    for j, copy in sorted(zip(Z_ORDER, z_copies), key=lambda e: min(e[0], NZ - e[0])):
        copy.wait_recv()
        block = block + z_recv[j]
    for o in range(3):
        head_ref[pl.ds(8 * o, 8), :] = (pltpu.roll(block, 128 - 36 * o, 1) if o else block)[:, :36]

    for copy in [*send_img, send_desc, send_ids, *a_copies, *handed, *p_copies, *y_copies, *z_copies]:
        copy.wait_send()

    @pl.when(helps)
    def _():
        carry.wait_send()

    text_copy.wait()
    image_copy.wait()


def placed(image_in, text_in, head_in, image_out, text_out, head_out, image, text, head, sem):
    pairs = [(head_in, head, head_out)]
    step = ROWS // PLACE_PARTS
    for n in range(PLACE_PARTS):
        rows = pl.ds(n * step, step)
        pairs.append((image_in.at[rows], image.at[rows], image_out.at[rows]))
        pairs.append((text_in.at[rows], text.at[rows], text_out.at[rows]))
    reads = [pltpu.make_async_copy(a, b, sem.at[0, n]) for n, (a, b, _) in enumerate(pairs)]
    writes = [pltpu.make_async_copy(b, c, sem.at[1, n]) for n, (_, b, c) in enumerate(pairs)]
    for copy in reads:
        copy.start()
    for read, write in zip(reads, writes):
        read.wait()
        write.start()
    for copy in writes:
        copy.wait()


def shards(img, desc, ids, w, dw, scale, bias):
    bf16, f32 = jnp.bfloat16, jnp.float32
    any_spec = pl.BlockSpec(memory_space=pl.ANY)
    dma = pltpu.SemaphoreType.DMA
    results = pl.pallas_call(
        kernel,
        out_shape=(
            jax.ShapeDtypeStruct((ROWS, D), bf16),
            jax.ShapeDtypeStruct((ROWS, D), bf16),
            jax.ShapeDtypeStruct((24, 36), f32),
        ),
        in_specs=[any_spec] * 5 + [pl.BlockSpec(memory_space=pltpu.SMEM)] * 2,
        out_specs=(any_spec, any_spec, pl.BlockSpec(memory_space=pltpu.VMEM)),
        scratch_shapes=[
            pltpu.VMEM((2 * ROWS, D), bf16),
            pltpu.VMEM((2 * ROWS, D), bf16),
            pltpu.VMEM((2 * ROWS, D), bf16),
            pltpu.VMEM((1, ROWS), jnp.int32),
            pltpu.VMEM((1, ROWS), jnp.int32),
            pltpu.VMEM((D, D), bf16),
            pltpu.VMEM((D, D), bf16),
            pltpu.VMEM((D, D), bf16),
            pltpu.VMEM((ROWS, D), f32),
            pltpu.VMEM((2 * ROWS, D), bf16),
            pltpu.VMEM((2, HEAD_COLS, ROWS), bf16),
            pltpu.VMEM((GROUP, HEAD_COLS, ROWS), bf16),
            pltpu.VMEM((NX, HEAD_COLS // NX, ROWS), bf16),
            pltpu.VMEM((GROUP, HEAD_COLS // NX, ROWS), bf16),
            pltpu.VMEM((HEAD_COLS, 256), f32),
            pltpu.VMEM((NY, 96, 128), f32),
            pltpu.VMEM((NY, 96, 128), bf16),
            pltpu.VMEM((NY, 96, 128), bf16),
            pltpu.VMEM((NZ, 8, 128), f32),
            pltpu.VMEM((NZ, 8, 128), f32),
            pltpu.VMEM((ROWS, D), bf16),
            pltpu.VMEM((ROWS, D), bf16),
            dma((4 + 2 * W_CHUNKS,)),
            dma((2,)),
            dma((5,)),
            dma((5,)),
            dma((GROUP,)),
            dma((GROUP,)),
            dma((GROUP,)),
            dma((GROUP,)),
            dma((NY,)),
            dma((NY,)),
            dma((NZ,)),
            dma((NZ,)),
            pltpu.SemaphoreType.REGULAR((6,)),
            pltpu.SemaphoreType.REGULAR,
            pltpu.VMEM((IMG_PARTS[1][1], D), bf16),
            dma,
            dma,
        ],
        compiler_params=pltpu.CompilerParams(
            collective_id=0, has_side_effects=True, vmem_limit_bytes=63 << 20
        ),
        name="contrastive",
    )(img, desc, ids.reshape(1, ROWS), w, dw, scale, bias)
    return pl.pallas_call(
        placed,
        out_shape=[jax.ShapeDtypeStruct(r.shape, r.dtype) for r in results],
        in_specs=[any_spec] * 3,
        out_specs=[any_spec] * 3,
        scratch_shapes=[
            *[pltpu.VMEM(r.shape, r.dtype) for r in results],
            dma((2, 2 * PLACE_PARTS + 1)),
        ],
        compiler_params=pltpu.CompilerParams(vmem_limit_bytes=63 << 20),
        name="placed",
    )(*results)


def solution(mesh):
    rows = P(("blk", "dp"), None)
    return jax.shard_map(
        shards,
        mesh=mesh,
        in_specs=(rows, rows, P(("blk", "dp")), P(), P(), P(), P()),
        out_specs=(rows, rows, P("blk", "dp")),
        check_vma=False,
    )
```

```python
import functools

import jax
import jax.numpy as jnp
from jax import lax
from jax.experimental import pallas as pl
from jax.experimental.pallas import tpu as pltpu
from jax.sharding import PartitionSpec as P

D = 1152
HEAD_COLS = 576
ROWS = 128
EPSILON = 1e-06
MESH = pl.DeviceIdType.MESH
NX, NY, NZ, NC, ZL = 4, 8, 12, 2, 4
GROUP = NX * NC
W_CHUNKS = 3
PLACE_PARTS = 4
IMG_PARTS = ((0, 64), (64, 32), (96, 32))
Y_ORDER = (4, 3, 5, 2, 6, 1, 7)
Z_ORDER = (6, 5, 7, 4, 8, 3, 9, 2, 10, 1, 11)
WC = D // W_CHUNKS


def device_at(x, y, z, c):
    x, y, z, c = lax.rem(x, NX), lax.rem(y, NY), lax.rem(z, NZ), lax.rem(c, NC)
    return ((z // ZL) * NY + y) * NC + c, x * ZL + lax.rem(z, ZL)


def coefficients(logits, ids, base):
    image_rows = base + lax.broadcasted_iota(jnp.int32, logits.shape, 0)
    match = image_rows == ids
    value = jax.nn.sigmoid(jnp.where(match, -logits, logits))
    return jnp.where(match, -value, value).astype(jnp.bfloat16)


def nt(left, right):
    return lax.dot_general(left, right, (((1,), (1,)), ((), ())), preferred_element_type=jnp.float32)


def tn(left, right):
    return lax.dot_general(left, right, (((0,), (0,)), ((), ())), preferred_element_type=jnp.float32)


def unit_scale(values):
    return lax.rsqrt(jnp.sum(values * values, axis=1, keepdims=True) + EPSILON)


def kernel(
    img_hbm, desc_hbm, ids_hbm, w_hbm, dw_hbm, scale_ref, bias_ref,
    image_out, text_out, head_ref,
    imgs, img_units, descs, ids, ids_prev, w, dw, pert, proj, text_unit,
    at_send, at_all, pt_send, pt_all, r_buf, y_own, y_send, y_recv, z_send, z_recv,
    local_sem, ring_send, ring_recv, a_send_sem, a_recv_sem, p_send_sem, p_recv_sem,
    y_send_sem, y_recv_sem, z_send_sem, z_recv_sem, word, ready, carried, help_recv, carry_send,
):
    b = lax.axis_index("blk")
    d = lax.axis_index("dp")
    c, y, z, x = lax.rem(b, 2), lax.rem(b // 2, NY), (b // (2 * NY)) * ZL + lax.rem(d, ZL), d // ZL
    after = (lax.rem(b + 1, 48), d)
    before = (lax.rem(b + 47, 48), d)
    group = [(i, f) for i in range(NX) for f in range(NC) if (i, f) != (0, 0)]

    barrier = pltpu.get_barrier_semaphore()
    for i, f in group:
        pl.semaphore_signal(barrier, inc=1, device_id=device_at(x + i, y, z, c + f), device_id_type=MESH)
    across = (lax.rem(b + 47 + 2 * c, 48), d)
    goes_out = jnp.logical_and(y == 0, c == 0)
    comes_in = jnp.logical_and(y == NY - 1, c == 1)
    helps = jnp.logical_and(jnp.logical_or(y == NY - 1, y == 1), c == 0)
    helpers = [device_at(x, NY - 1, z + ZL, 0), device_at(x, 1, z + ZL, 0)]

    @pl.when(jnp.logical_not(goes_out))
    def _():
        pl.semaphore_signal(barrier, inc=1, device_id=across, device_id_type=MESH)

    @pl.when(comes_in)
    def _():
        for helper in helpers:
            pl.semaphore_signal(barrier, inc=1, device_id=helper, device_id_type=MESH)

    for j in (1, NY - 1):
        pl.semaphore_signal(barrier, inc=1, device_id=device_at(x, y + j, z, c), device_id_type=MESH)
    for j in (1, NZ - 1):
        pl.semaphore_signal(barrier, inc=1, device_id=device_at(x, y, z + j, c), device_id_type=MESH)

    loads = [
        pltpu.make_async_copy(desc_hbm, descs.at[pl.ds(0, ROWS)], local_sem.at[0]),
        pltpu.make_async_copy(img_hbm, imgs.at[pl.ds(0, ROWS)], local_sem.at[1]),
        pltpu.make_async_copy(ids_hbm, ids, local_sem.at[2]),
    ]
    for copy in loads:
        copy.start()
    w_loads = []
    for n in range(W_CHUNKS):
        cols = pl.ds(n * WC, WC)
        pair = [
            pltpu.make_async_copy(w_hbm.at[:, cols], w.at[:, cols], local_sem.at[3 + 2 * n]),
            pltpu.make_async_copy(dw_hbm.at[:, cols], dw.at[:, cols], local_sem.at[4 + 2 * n]),
        ]
        for copy in pair:
            copy.start()
        w_loads.append(pair)

    loads[0].wait()
    desc = descs[pl.ds(0, ROWS), :]
    turned = jnp.transpose(desc.astype(jnp.float32)).reshape(24, 2, 24, ROWS)
    for parity in range(2):
        at_send[parity] = turned[:, parity].reshape(HEAD_COLS, ROWS).astype(jnp.bfloat16)
    for copy in loads[1:]:
        copy.wait()

    pl.semaphore_wait(barrier, len(group) + 4 + jnp.where(comes_in, 0, 1) + jnp.where(helps, 1, 0))

    def pass_on(round_, along_y, along_z):
        for j in along_y:
            pl.semaphore_signal(
                word.at[2 * round_], inc=1, device_id=device_at(x, y + j, z, c), device_id_type=MESH
            )
        for j in along_z:
            pl.semaphore_signal(
                word.at[2 * round_ + 1], inc=1, device_id=device_at(x, y, z + j, c), device_id_type=MESH
            )

    pass_on(0, (1, NY - 1), (1, NZ - 1))

    def remote(src, dst, send, recv, device):
        return pltpu.make_async_remote_copy(
            src_ref=src, dst_ref=dst, send_sem=send, recv_sem=recv, device_id=device, device_id_type=MESH
        )

    def img_part(part, device):
        rows, n = IMG_PARTS[part]
        return remote(
            imgs.at[pl.ds(rows, n)], imgs.at[pl.ds(ROWS + rows, n)], ring_send.at[part], ring_recv.at[part], device
        )

    def help_part(part, device):
        rows, n = IMG_PARTS[part]
        return remote(imgs.at[pl.ds(rows, n)], carried, ring_send.at[part], help_recv, device)

    send_img = [img_part(part, before) for part in range(3)]

    @pl.when(goes_out)
    def _():
        pl.semaphore_signal(ready, inc=1, device_id=across, device_id_type=MESH)
        help_part(1, device_at(x, NY - 1, z, 0)).start()
        help_part(2, device_at(x, 1, z, 0)).start()
        send_img[0].start()

    @pl.when(jnp.logical_not(goes_out))
    def _():
        for copy in send_img:
            copy.start()

    def slot(i, core):
        return i * NC + core

    first = jnp.where(c == 0, NX - 1, 1)
    a_copies = []
    for n, (i, f) in enumerate([(first, 0), (first, 1), (0, 1), (NX - first, 0), (NX - first, 1)]):
        copy = remote(
            at_send.at[lax.rem(c + f, NC)], at_all.at[slot(i, c)],
            a_send_sem.at[n], a_recv_sem.at[slot(i, c)], device_at(x + i, y, z, c + f),
        )
        copy.start()
        a_copies.append(copy)

    def a_arrived(s):
        return remote(at_send.at[0], at_all.at[s], a_send_sem.at[0], a_recv_sem.at[s], before)

    def p_arrived(s):
        return remote(pt_send.at[0], pt_all.at[s], p_send_sem.at[0], p_recv_sem.at[s], before)

    for n in range(W_CHUNKS):
        cols = pl.ds(n * WC, WC)
        for copy in w_loads[n]:
            copy.wait()
        part = (w[:, cols].astype(jnp.float32) + dw[:, cols].astype(jnp.float32)).astype(jnp.bfloat16)
        pert[:, cols] = part
        proj[:, cols] = jnp.dot(descs[pl.ds(0, ROWS), :], part, preferred_element_type=jnp.float32)
    pl.semaphore_wait(word.at[0], 2)
    pl.semaphore_wait(word.at[1], 2)
    pass_on(1, (2, NY - 2), (2, NZ - 2))

    projected = proj[...]
    text_scale = unit_scale(projected)
    unit = projected * text_scale
    proj[...] = unit
    text_unit[pl.ds(0, ROWS), :] = unit.astype(jnp.bfloat16)

    img = imgs[pl.ds(0, ROWS), :].astype(jnp.float32)
    image_scale = unit_scale(img)
    img_units[pl.ds(0, ROWS), :] = (img * image_scale).astype(jnp.bfloat16)
    at_all[slot(0, c)] = at_send[c]

    carry = remote(
        carried,
        imgs.at[pl.ds(ROWS + IMG_PARTS[1][0] + jnp.where(y == 1, IMG_PARTS[1][1], 0), IMG_PARTS[1][1])],
        carry_send, ring_recv.at[jnp.where(y == 1, 2, 1)], device_at(x, NY - 1, z + NZ - ZL, 1),
    )

    @pl.when(helps)
    def _():
        help_part(1, before).wait_recv()
        carry.start()

    @pl.when(comes_in)
    def _():
        pl.semaphore_wait(ready, 1)

    send_desc = remote(descs.at[pl.ds(0, ROWS)], descs.at[pl.ds(ROWS, ROWS)], ring_send.at[3], ring_recv.at[3], after)
    send_ids = remote(ids, ids_prev, ring_send.at[4], ring_recv.at[4], after)
    send_desc.start()
    send_ids.start()

    handed = []
    for n, (i, core) in enumerate([(NX - 1, 0), (1, 1)]):
        a_arrived(slot(i, core)).wait_recv()
        copy = remote(
            at_all.at[slot(i, core)], at_all.at[slot(2, core)],
            a_send_sem.at[5 + n], a_recv_sem.at[slot(2, core)], device_at(x + i, y, z, c),
        )
        copy.start()
        handed.append(copy)

    scale = scale_ref[...]
    bias = bias_ref[...]
    row_base = (b * 16 + d) * ROWS
    next_base = (after[0] * 16 + d) * ROWS

    for copy in send_img:
        copy.wait_recv()
    img_next = imgs[pl.ds(ROWS, ROWS), :].astype(jnp.float32)
    img_units[pl.ds(ROWS, ROWS), :] = (img_next * unit_scale(img_next)).astype(jnp.bfloat16)
    logits = scale * nt(img_units[...], text_unit[pl.ds(0, ROWS), :]) + bias
    my_ids = ids[...]
    coef_own = coefficients(logits[:ROWS], my_ids, row_base)
    coef_next = coefficients(logits[ROWS:], my_ids, next_base)
    unit_text_grad = scale * tn(jnp.concatenate([coef_own, coef_next], axis=0), img_units[...])
    along = jnp.sum(unit * unit_text_grad, axis=1, keepdims=True)
    pre_grad = text_scale * (unit_text_grad - unit * along)
    pt = jnp.transpose(pre_grad[:, :HEAD_COLS])
    pt_send[...] = pt.reshape(NX, HEAD_COLS // NX, ROWS).astype(jnp.bfloat16)
    p_copies = []
    for n, (i, f) in enumerate([(2, 0), (2, 1), (1, 0), (1, 1), (3, 0), (3, 1), (0, 1)]):
        copy = remote(
            pt_send.at[lax.rem(x + i, NX)], pt_all.at[slot(i, c)],
            p_send_sem.at[n], p_recv_sem.at[slot(i, c)], device_at(x + i, y, z, c + f),
        )
        copy.start()
        p_copies.append(copy)
    pt_all[slot(0, c)] = pt_send[x]

    pl.semaphore_wait(word.at[2], 2)
    pl.semaphore_wait(word.at[3], 2)
    pass_on(2, (), (2, NZ - 2))

    text_out[...] = nt(pre_grad.astype(jnp.bfloat16), pert[...]).astype(jnp.bfloat16)

    for i in range(NX):
        for core in range(NC):
            if i in (1, 2, 3) and (i, core) not in ((NX - 1, 0), (1, 1)):
                a_arrived(slot(i, core)).wait_recv()
            if i:
                p_arrived(slot(i, core)).wait_recv()
    a_arrived(slot(0, 1 - c)).wait_recv()
    p_arrived(slot(0, 1 - c)).wait_recv()
    features = jnp.concatenate([at_all[s] for s in range(GROUP)], axis=1)
    columns = jnp.concatenate([pt_all[s] for s in range(GROUP)], axis=1)
    r_buf[:, pl.ds(0, 144)] = nt(features, columns)
    low = r_buf[:, pl.ds(0, 128)].reshape(24, 3, 8, 128)
    high = r_buf[:, pl.ds(128, 128)].reshape(24, 3, 8, 128)
    lane = lax.broadcasted_iota(jnp.int32, (24, 8, 128), 2)

    def moved(values, shift):
        shift = shift % 128
        return pltpu.roll(values, shift, 2) if shift else values

    for k in range(ZL):
        parts = []
        for o in range(3):
            part = moved(low[:, o], 36 * o - 36 * k)
            if k == ZL - 1:
                part = jnp.where(lane < 36 * o + 20, part, moved(high[:, o], 36 * o + 20))
            parts.append(part)
        tile = jnp.where(lane < 36, parts[0], jnp.where(lane < 72, parts[1], parts[2]))
        tile = jnp.where(lane < 108, tile, 0.0).reshape(3, NY, 8, 128)
        for h in range(3):
            y_own[:, pl.ds((h * ZL + k) * 8, 8), :] = tile[h]
    y_send[...] = y_own[...].astype(jnp.bfloat16)
    y_copies = []
    for j in Y_ORDER:
        copy = remote(
            y_send.at[lax.rem(y + j, NY)], y_recv.at[j], y_send_sem.at[j], y_recv_sem.at[j], device_at(x, y + j, z, c)
        )
        copy.start()
        y_copies.append(copy)

    total = y_own[y]
    for j, copy in sorted(zip(Y_ORDER, y_copies), key=lambda e: min(e[0], NY - e[0])):
        copy.wait_recv()
        total = total + y_recv[j].astype(jnp.float32)
    pl.semaphore_wait(word.at[5], 2)
    z_send[...] = total.reshape(NZ, 8, 128)
    z_copies = []
    for j in Z_ORDER:
        copy = remote(
            z_send.at[lax.rem(z + j, NZ)], z_recv.at[j], z_send_sem.at[j], z_recv_sem.at[j], device_at(x, y, z + j, c)
        )
        copy.start()
        z_copies.append(copy)
    send_desc.wait_recv()
    send_ids.wait_recv()
    projected_prev = jnp.dot(descs[pl.ds(ROWS, ROWS), :], pert[...], preferred_element_type=jnp.float32)
    text_unit[pl.ds(ROWS, ROWS), :] = (projected_prev * unit_scale(projected_prev)).astype(jnp.bfloat16)
    logits_prev = scale * nt(img_units[pl.ds(0, ROWS), :], text_unit[pl.ds(ROWS, ROWS), :]) + bias
    coef_prev = coefficients(logits_prev, ids_prev[...], row_base)
    unit_image_grad = scale * jnp.dot(
        jnp.concatenate([coef_own, coef_prev], axis=1), text_unit[...], preferred_element_type=jnp.float32
    )
    img = imgs[pl.ds(0, ROWS), :].astype(jnp.float32)
    image_dir = img * image_scale
    along_image = jnp.sum(image_dir * unit_image_grad, axis=1, keepdims=True)
    image_out[...] = (image_scale * (unit_image_grad - image_dir * along_image)).astype(jnp.bfloat16)

    block = z_send[z]
    for j, copy in sorted(zip(Z_ORDER, z_copies), key=lambda e: min(e[0], NZ - e[0])):
        copy.wait_recv()
        block = block + z_recv[j]
    for o in range(3):
        head_ref[pl.ds(8 * o, 8), :] = (pltpu.roll(block, 128 - 36 * o, 1) if o else block)[:, :36]

    for copy in [*send_img, send_desc, send_ids, *a_copies, *handed, *p_copies, *y_copies, *z_copies]:
        copy.wait_send()

    @pl.when(helps)
    def _():
        carry.wait_send()


def placed(image_in, text_in, head_in, image_out, text_out, head_out, sem):
    copies = [pltpu.make_async_copy(head_in, head_out, sem.at[2 * PLACE_PARTS])]
    step = ROWS // PLACE_PARTS
    for n in range(PLACE_PARTS):
        rows = pl.ds(n * step, step)
        copies.append(pltpu.make_async_copy(image_in.at[rows], image_out.at[rows], sem.at[2 * n]))
        copies.append(pltpu.make_async_copy(text_in.at[rows], text_out.at[rows], sem.at[2 * n + 1]))
    for copy in copies:
        copy.start()
    for copy in copies:
        copy.wait()


def shards(img, desc, ids, w, dw, scale, bias):
    bf16, f32 = jnp.bfloat16, jnp.float32
    any_spec = pl.BlockSpec(memory_space=pl.ANY)
    dma = pltpu.SemaphoreType.DMA
    results = pl.pallas_call(
        kernel,
        out_shape=(
            pltpu.VMEM((ROWS, D), bf16),
            pltpu.VMEM((ROWS, D), bf16),
            pltpu.VMEM((24, 36), f32),
        ),
        in_specs=[any_spec] * 5 + [pl.BlockSpec(memory_space=pltpu.SMEM)] * 2,
        out_specs=(pl.BlockSpec(memory_space=pltpu.VMEM),) * 3,
        scratch_shapes=[
            pltpu.VMEM((2 * ROWS, D), bf16),
            pltpu.VMEM((2 * ROWS, D), bf16),
            pltpu.VMEM((2 * ROWS, D), bf16),
            pltpu.VMEM((1, ROWS), jnp.int32),
            pltpu.VMEM((1, ROWS), jnp.int32),
            pltpu.VMEM((D, D), bf16),
            pltpu.VMEM((D, D), bf16),
            pltpu.VMEM((D, D), bf16),
            pltpu.VMEM((ROWS, D), f32),
            pltpu.VMEM((2 * ROWS, D), bf16),
            pltpu.VMEM((2, HEAD_COLS, ROWS), bf16),
            pltpu.VMEM((GROUP, HEAD_COLS, ROWS), bf16),
            pltpu.VMEM((NX, HEAD_COLS // NX, ROWS), bf16),
            pltpu.VMEM((GROUP, HEAD_COLS // NX, ROWS), bf16),
            pltpu.VMEM((HEAD_COLS, 256), f32),
            pltpu.VMEM((NY, 96, 128), f32),
            pltpu.VMEM((NY, 96, 128), bf16),
            pltpu.VMEM((NY, 96, 128), bf16),
            pltpu.VMEM((NZ, 8, 128), f32),
            pltpu.VMEM((NZ, 8, 128), f32),
            dma((4 + 2 * W_CHUNKS,)),
            dma((5,)),
            dma((5,)),
            dma((GROUP,)),
            dma((GROUP,)),
            dma((GROUP,)),
            dma((GROUP,)),
            dma((NY,)),
            dma((NY,)),
            dma((NZ,)),
            dma((NZ,)),
            pltpu.SemaphoreType.REGULAR((6,)),
            pltpu.SemaphoreType.REGULAR,
            pltpu.VMEM((IMG_PARTS[1][1], D), bf16),
            dma,
            dma,
        ],
        compiler_params=pltpu.CompilerParams(
            collective_id=0, has_side_effects=True, vmem_limit_bytes=56 << 20
        ),
        name="contrastive",
    )(*(pltpu.with_memory_space_constraint(v, pltpu.HBM) for v in (img, desc, ids.reshape(1, ROWS), w, dw)), scale, bias)
    return pl.pallas_call(
        placed,
        out_shape=[jax.ShapeDtypeStruct(r.shape, r.dtype) for r in results],
        in_specs=[any_spec] * 3,
        out_specs=[any_spec] * 3,
        scratch_shapes=[
            dma((2 * PLACE_PARTS + 1,)),
        ],
        compiler_params=pltpu.CompilerParams(vmem_limit_bytes=4 << 20),
        name="placed",
    )(*results)


def solution(mesh):
    rows = P(("blk", "dp"), None)
    return jax.shard_map(
        shards,
        mesh=mesh,
        in_specs=(rows, rows, P(("blk", "dp")), P(), P(), P(), P()),
        out_specs=(rows, rows, P("blk", "dp")),
        check_vma=False,
    )
```

```python
import functools

import jax
import jax.numpy as jnp
from jax import lax
from jax.experimental import pallas as pl
from jax.experimental.pallas import tpu as pltpu
from jax.sharding import PartitionSpec as P

D = 1152
HEAD_COLS = 576
ROWS = 128
EPSILON = 1e-06
MESH = pl.DeviceIdType.MESH
NX, NY, NZ, NC, ZL = 4, 8, 12, 2, 4
GROUP = NX * NC
W_CHUNKS = 3
PLACE_PARTS = 2
IMG_PARTS = ((0, 64), (64, 32), (96, 32))
Y_ORDER = (4, 3, 5, 2, 6, 1, 7)
Z_ORDER = (6, 5, 7, 4, 8, 3, 9, 2, 10, 1, 11)
WC = D // W_CHUNKS


def device_at(x, y, z, c):
    x, y, z, c = lax.rem(x, NX), lax.rem(y, NY), lax.rem(z, NZ), lax.rem(c, NC)
    return ((z // ZL) * NY + y) * NC + c, x * ZL + lax.rem(z, ZL)


def coefficients(logits, ids, base):
    image_rows = base + lax.broadcasted_iota(jnp.int32, logits.shape, 0)
    match = image_rows == ids
    value = jax.nn.sigmoid(jnp.where(match, -logits, logits))
    return jnp.where(match, -value, value).astype(jnp.bfloat16)


def nt(left, right):
    return lax.dot_general(left, right, (((1,), (1,)), ((), ())), preferred_element_type=jnp.float32)


def tn(left, right):
    return lax.dot_general(left, right, (((0,), (0,)), ((), ())), preferred_element_type=jnp.float32)


def unit_scale(values):
    return lax.rsqrt(jnp.sum(values * values, axis=1, keepdims=True) + EPSILON)


def kernel(
    img_hbm, desc_hbm, ids_hbm, w_hbm, dw_hbm, scale_ref, bias_ref,
    image_out, text_out, head_ref,
    imgs, img_units, descs, ids, ids_prev, w, dw, pert, proj, text_unit,
    at_send, at_all, pt_send, pt_all, r_buf, y_own, y_send, y_recv, z_send, z_recv,
    local_sem, ring_send, ring_recv, a_send_sem, a_recv_sem, p_send_sem, p_recv_sem,
    y_send_sem, y_recv_sem, z_send_sem, z_recv_sem, word, ready, carried, help_recv, carry_send,
):
    b = lax.axis_index("blk")
    d = lax.axis_index("dp")
    c, y, z, x = lax.rem(b, 2), lax.rem(b // 2, NY), (b // (2 * NY)) * ZL + lax.rem(d, ZL), d // ZL
    after = (lax.rem(b + 1, 48), d)
    before = (lax.rem(b + 47, 48), d)
    group = [(i, f) for i in range(NX) for f in range(NC) if (i, f) != (0, 0)]

    barrier = pltpu.get_barrier_semaphore()
    for i, f in group:
        pl.semaphore_signal(barrier, inc=1, device_id=device_at(x + i, y, z, c + f), device_id_type=MESH)
    across = (lax.rem(b + 47 + 2 * c, 48), d)
    goes_out = jnp.logical_and(y == 0, c == 0)
    comes_in = jnp.logical_and(y == NY - 1, c == 1)
    helps = jnp.logical_and(jnp.logical_or(y == NY - 1, y == 1), c == 0)
    helpers = [device_at(x, NY - 1, z + ZL, 0), device_at(x, 1, z + ZL, 0)]

    @pl.when(jnp.logical_not(goes_out))
    def _():
        pl.semaphore_signal(barrier, inc=1, device_id=across, device_id_type=MESH)

    @pl.when(comes_in)
    def _():
        for helper in helpers:
            pl.semaphore_signal(barrier, inc=1, device_id=helper, device_id_type=MESH)

    for j in (1, NY - 1):
        pl.semaphore_signal(barrier, inc=1, device_id=device_at(x, y + j, z, c), device_id_type=MESH)
    for j in (1, NZ - 1):
        pl.semaphore_signal(barrier, inc=1, device_id=device_at(x, y, z + j, c), device_id_type=MESH)

    loads = [
        pltpu.make_async_copy(desc_hbm, descs.at[pl.ds(0, ROWS)], local_sem.at[0]),
        pltpu.make_async_copy(img_hbm, imgs.at[pl.ds(0, ROWS)], local_sem.at[1]),
        pltpu.make_async_copy(ids_hbm, ids, local_sem.at[2]),
    ]
    for copy in loads:
        copy.start()
    w_loads = []
    for n in range(W_CHUNKS):
        cols = pl.ds(n * WC, WC)
        pair = [
            pltpu.make_async_copy(w_hbm.at[:, cols], w.at[:, cols], local_sem.at[3 + 2 * n]),
            pltpu.make_async_copy(dw_hbm.at[:, cols], dw.at[:, cols], local_sem.at[4 + 2 * n]),
        ]
        for copy in pair:
            copy.start()
        w_loads.append(pair)

    loads[0].wait()
    desc = descs[pl.ds(0, ROWS), :]
    turned = jnp.transpose(desc.astype(jnp.float32)).reshape(24, 2, 24, ROWS)
    for parity in range(2):
        at_send[parity] = turned[:, parity].reshape(HEAD_COLS, ROWS).astype(jnp.bfloat16)
    for copy in loads[1:]:
        copy.wait()

    pl.semaphore_wait(barrier, len(group) + 4 + jnp.where(comes_in, 0, 1) + jnp.where(helps, 1, 0))

    def pass_on(round_, along_y, along_z):
        for j in along_y:
            pl.semaphore_signal(
                word.at[2 * round_], inc=1, device_id=device_at(x, y + j, z, c), device_id_type=MESH
            )
        for j in along_z:
            pl.semaphore_signal(
                word.at[2 * round_ + 1], inc=1, device_id=device_at(x, y, z + j, c), device_id_type=MESH
            )

    pass_on(0, (1, NY - 1), (1, NZ - 1))

    def remote(src, dst, send, recv, device):
        return pltpu.make_async_remote_copy(
            src_ref=src, dst_ref=dst, send_sem=send, recv_sem=recv, device_id=device, device_id_type=MESH
        )

    def img_part(part, device):
        rows, n = IMG_PARTS[part]
        return remote(
            imgs.at[pl.ds(rows, n)], imgs.at[pl.ds(ROWS + rows, n)], ring_send.at[part], ring_recv.at[part], device
        )

    def help_part(part, device):
        rows, n = IMG_PARTS[part]
        return remote(imgs.at[pl.ds(rows, n)], carried, ring_send.at[part], help_recv, device)

    send_img = [img_part(part, before) for part in range(3)]

    @pl.when(goes_out)
    def _():
        pl.semaphore_signal(ready, inc=1, device_id=across, device_id_type=MESH)
        help_part(1, device_at(x, NY - 1, z, 0)).start()
        help_part(2, device_at(x, 1, z, 0)).start()
        send_img[0].start()

    def slot(i, core):
        return i * NC + core

    first = jnp.where(c == 0, NX - 1, 1)
    a_copies = []
    for n, (i, f) in enumerate([(first, 0), (first, 1), (0, 1), (NX - first, 0), (NX - first, 1)]):
        copy = remote(
            at_send.at[lax.rem(c + f, NC)], at_all.at[slot(i, c)],
            a_send_sem.at[n], a_recv_sem.at[slot(i, c)], device_at(x + i, y, z, c + f),
        )
        copy.start()
        a_copies.append(copy)

    @pl.when(jnp.logical_not(goes_out))
    def _():
        for copy in send_img:
            copy.start()

    def a_arrived(s):
        return remote(at_send.at[0], at_all.at[s], a_send_sem.at[0], a_recv_sem.at[s], before)

    def p_arrived(s):
        return remote(pt_send.at[0], pt_all.at[s], p_send_sem.at[0], p_recv_sem.at[s], before)

    for n in range(W_CHUNKS):
        cols = pl.ds(n * WC, WC)
        for copy in w_loads[n]:
            copy.wait()
        part = (w[:, cols].astype(jnp.float32) + dw[:, cols].astype(jnp.float32)).astype(jnp.bfloat16)
        pert[:, cols] = part
        proj[:, cols] = jnp.dot(descs[pl.ds(0, ROWS), :], part, preferred_element_type=jnp.float32)
    pl.semaphore_wait(word.at[0], 2)
    pl.semaphore_wait(word.at[1], 2)
    pass_on(1, (2, NY - 2), (2, NZ - 2))

    projected = proj[...]
    text_scale = unit_scale(projected)
    unit = projected * text_scale
    proj[...] = unit
    text_unit[pl.ds(0, ROWS), :] = unit.astype(jnp.bfloat16)

    img = imgs[pl.ds(0, ROWS), :].astype(jnp.float32)
    image_scale = unit_scale(img)
    img_units[pl.ds(0, ROWS), :] = (img * image_scale).astype(jnp.bfloat16)
    at_all[slot(0, c)] = at_send[c]

    carry = remote(
        carried,
        imgs.at[pl.ds(ROWS + IMG_PARTS[1][0] + jnp.where(y == 1, IMG_PARTS[1][1], 0), IMG_PARTS[1][1])],
        carry_send, ring_recv.at[jnp.where(y == 1, 2, 1)], device_at(x, NY - 1, z + NZ - ZL, 1),
    )

    @pl.when(helps)
    def _():
        help_part(1, before).wait_recv()
        carry.start()

    @pl.when(comes_in)
    def _():
        pl.semaphore_wait(ready, 1)

    send_desc = remote(descs.at[pl.ds(0, ROWS)], descs.at[pl.ds(ROWS, ROWS)], ring_send.at[3], ring_recv.at[3], after)
    send_ids = remote(ids, ids_prev, ring_send.at[4], ring_recv.at[4], after)
    send_desc.start()
    send_ids.start()

    handed = []
    for n, (i, core) in enumerate([(NX - 1, 0), (1, 1)]):
        a_arrived(slot(i, core)).wait_recv()
        copy = remote(
            at_all.at[slot(i, core)], at_all.at[slot(2, core)],
            a_send_sem.at[5 + n], a_recv_sem.at[slot(2, core)], device_at(x + i, y, z, c),
        )
        copy.start()
        handed.append(copy)

    scale = scale_ref[...]
    bias = bias_ref[...]
    row_base = (b * 16 + d) * ROWS
    next_base = (after[0] * 16 + d) * ROWS

    for copy in send_img:
        copy.wait_recv()
    img_next = imgs[pl.ds(ROWS, ROWS), :].astype(jnp.float32)
    img_units[pl.ds(ROWS, ROWS), :] = (img_next * unit_scale(img_next)).astype(jnp.bfloat16)
    logits = scale * nt(img_units[...], text_unit[pl.ds(0, ROWS), :]) + bias
    my_ids = ids[...]
    coef_own = coefficients(logits[:ROWS], my_ids, row_base)
    coef_next = coefficients(logits[ROWS:], my_ids, next_base)
    unit_text_grad = scale * tn(jnp.concatenate([coef_own, coef_next], axis=0), img_units[...])
    along = jnp.sum(unit * unit_text_grad, axis=1, keepdims=True)
    pre_grad = text_scale * (unit_text_grad - unit * along)
    pt = jnp.transpose(pre_grad[:, :HEAD_COLS])
    pt_send[...] = pt.reshape(NX, HEAD_COLS // NX, ROWS).astype(jnp.bfloat16)
    p_copies = []
    for n, (i, f) in enumerate([(2, 0), (2, 1), (1, 0), (1, 1), (3, 0), (3, 1), (0, 1)]):
        copy = remote(
            pt_send.at[lax.rem(x + i, NX)], pt_all.at[slot(i, c)],
            p_send_sem.at[n], p_recv_sem.at[slot(i, c)], device_at(x + i, y, z, c + f),
        )
        copy.start()
        p_copies.append(copy)
    pt_all[slot(0, c)] = pt_send[x]

    pl.semaphore_wait(word.at[2], 2)
    pl.semaphore_wait(word.at[3], 2)
    pass_on(2, (), (2, NZ - 2))

    text_out[...] = nt(pre_grad.astype(jnp.bfloat16), pert[...]).astype(jnp.bfloat16)

    def product(slots):
        features = jnp.concatenate([at_all[s] for s in slots], axis=1)
        columns = jnp.concatenate([pt_all[s] for s in slots], axis=1)
        return nt(features, columns)

    a_arrived(slot(0, 1 - c)).wait_recv()
    p_arrived(slot(0, 1 - c)).wait_recv()
    for i in (1, NX - 1):
        for core in range(NC):
            if (i, core) not in ((NX - 1, 0), (1, 1)):
                a_arrived(slot(i, core)).wait_recv()
            p_arrived(slot(i, core)).wait_recv()
    r_buf[:, pl.ds(0, 144)] = product([slot(i, core) for i in (0, 1, NX - 1) for core in range(NC)])
    for core in range(NC):
        a_arrived(slot(2, core)).wait_recv()
        p_arrived(slot(2, core)).wait_recv()
    r_buf[:, pl.ds(0, 144)] += product([slot(2, core) for core in range(NC)])
    low = r_buf[:, pl.ds(0, 128)].reshape(24, 3, 8, 128)
    high = r_buf[:, pl.ds(128, 128)].reshape(24, 3, 8, 128)
    lane = lax.broadcasted_iota(jnp.int32, (24, 8, 128), 2)

    def moved(values, shift):
        shift = shift % 128
        return pltpu.roll(values, shift, 2) if shift else values

    for k in range(ZL):
        parts = []
        for o in range(3):
            part = moved(low[:, o], 36 * o - 36 * k)
            if k == ZL - 1:
                part = jnp.where(lane < 36 * o + 20, part, moved(high[:, o], 36 * o + 20))
            parts.append(part)
        tile = jnp.where(lane < 36, parts[0], jnp.where(lane < 72, parts[1], parts[2]))
        tile = jnp.where(lane < 108, tile, 0.0).reshape(3, NY, 8, 128)
        for h in range(3):
            y_own[:, pl.ds((h * ZL + k) * 8, 8), :] = tile[h]
    y_send[...] = y_own[...].astype(jnp.bfloat16)
    y_copies = []
    for j in Y_ORDER:
        copy = remote(
            y_send.at[lax.rem(y + j, NY)], y_recv.at[j], y_send_sem.at[j], y_recv_sem.at[j], device_at(x, y + j, z, c)
        )
        copy.start()
        y_copies.append(copy)

    total = y_own[y]
    for j, copy in sorted(zip(Y_ORDER, y_copies), key=lambda e: min(e[0], NY - e[0])):
        copy.wait_recv()
        total = total + y_recv[j].astype(jnp.float32)
    pl.semaphore_wait(word.at[5], 2)
    z_send[...] = total.reshape(NZ, 8, 128)
    z_copies = []
    for j in Z_ORDER:
        copy = remote(
            z_send.at[lax.rem(z + j, NZ)], z_recv.at[j], z_send_sem.at[j], z_recv_sem.at[j], device_at(x, y, z + j, c)
        )
        copy.start()
        z_copies.append(copy)
    send_desc.wait_recv()
    send_ids.wait_recv()
    projected_prev = jnp.dot(descs[pl.ds(ROWS, ROWS), :], pert[...], preferred_element_type=jnp.float32)
    text_unit[pl.ds(ROWS, ROWS), :] = (projected_prev * unit_scale(projected_prev)).astype(jnp.bfloat16)
    logits_prev = scale * nt(img_units[pl.ds(0, ROWS), :], text_unit[pl.ds(ROWS, ROWS), :]) + bias
    coef_prev = coefficients(logits_prev, ids_prev[...], row_base)
    unit_image_grad = scale * jnp.dot(
        jnp.concatenate([coef_own, coef_prev], axis=1), text_unit[...], preferred_element_type=jnp.float32
    )
    img = imgs[pl.ds(0, ROWS), :].astype(jnp.float32)
    image_dir = img * image_scale
    along_image = jnp.sum(image_dir * unit_image_grad, axis=1, keepdims=True)
    image_out[...] = (image_scale * (unit_image_grad - image_dir * along_image)).astype(jnp.bfloat16)

    block = z_send[z]
    for j, copy in sorted(zip(Z_ORDER, z_copies), key=lambda e: min(e[0], NZ - e[0])):
        copy.wait_recv()
        block = block + z_recv[j]
    for o in range(3):
        head_ref[pl.ds(8 * o, 8), :] = (pltpu.roll(block, 128 - 36 * o, 1) if o else block)[:, :36]

    for copy in [*send_img, send_desc, send_ids, *a_copies, *handed, *p_copies, *y_copies, *z_copies]:
        copy.wait_send()

    @pl.when(helps)
    def _():
        carry.wait_send()


def placed(image_in, text_in, head_in, image_out, text_out, head_out, sem):
    copies = [pltpu.make_async_copy(head_in, head_out, sem.at[2 * PLACE_PARTS])]
    step = ROWS // PLACE_PARTS
    for n in range(PLACE_PARTS):
        rows = pl.ds(n * step, step)
        copies.append(pltpu.make_async_copy(image_in.at[rows], image_out.at[rows], sem.at[2 * n]))
        copies.append(pltpu.make_async_copy(text_in.at[rows], text_out.at[rows], sem.at[2 * n + 1]))
    for copy in copies:
        copy.start()
    for copy in copies:
        copy.wait()


def shards(img, desc, ids, w, dw, scale, bias):
    bf16, f32 = jnp.bfloat16, jnp.float32
    any_spec = pl.BlockSpec(memory_space=pl.ANY)
    dma = pltpu.SemaphoreType.DMA
    results = pl.pallas_call(
        kernel,
        out_shape=(
            pltpu.VMEM((ROWS, D), bf16),
            pltpu.VMEM((ROWS, D), bf16),
            pltpu.VMEM((24, 36), f32),
        ),
        in_specs=[any_spec] * 5 + [pl.BlockSpec(memory_space=pltpu.SMEM)] * 2,
        out_specs=(pl.BlockSpec(memory_space=pltpu.VMEM),) * 3,
        scratch_shapes=[
            pltpu.VMEM((2 * ROWS, D), bf16),
            pltpu.VMEM((2 * ROWS, D), bf16),
            pltpu.VMEM((2 * ROWS, D), bf16),
            pltpu.VMEM((1, ROWS), jnp.int32),
            pltpu.VMEM((1, ROWS), jnp.int32),
            pltpu.VMEM((D, D), bf16),
            pltpu.VMEM((D, D), bf16),
            pltpu.VMEM((D, D), bf16),
            pltpu.VMEM((ROWS, D), f32),
            pltpu.VMEM((2 * ROWS, D), bf16),
            pltpu.VMEM((2, HEAD_COLS, ROWS), bf16),
            pltpu.VMEM((GROUP, HEAD_COLS, ROWS), bf16),
            pltpu.VMEM((NX, HEAD_COLS // NX, ROWS), bf16),
            pltpu.VMEM((GROUP, HEAD_COLS // NX, ROWS), bf16),
            pltpu.VMEM((HEAD_COLS, 256), f32),
            pltpu.VMEM((NY, 96, 128), f32),
            pltpu.VMEM((NY, 96, 128), bf16),
            pltpu.VMEM((NY, 96, 128), bf16),
            pltpu.VMEM((NZ, 8, 128), f32),
            pltpu.VMEM((NZ, 8, 128), f32),
            dma((4 + 2 * W_CHUNKS,)),
            dma((5,)),
            dma((5,)),
            dma((GROUP,)),
            dma((GROUP,)),
            dma((GROUP,)),
            dma((GROUP,)),
            dma((NY,)),
            dma((NY,)),
            dma((NZ,)),
            dma((NZ,)),
            pltpu.SemaphoreType.REGULAR((6,)),
            pltpu.SemaphoreType.REGULAR,
            pltpu.VMEM((IMG_PARTS[1][1], D), bf16),
            dma,
            dma,
        ],
        compiler_params=pltpu.CompilerParams(
            collective_id=0, has_side_effects=True, vmem_limit_bytes=56 << 20
        ),
        name="contrastive",
    )(*(pltpu.with_memory_space_constraint(v, pltpu.HBM) for v in (img, desc, ids.reshape(1, ROWS), w, dw)), scale, bias)
    return pl.pallas_call(
        placed,
        out_shape=[jax.ShapeDtypeStruct(r.shape, r.dtype) for r in results],
        in_specs=[any_spec] * 3,
        out_specs=[any_spec] * 3,
        scratch_shapes=[
            dma((2 * PLACE_PARTS + 1,)),
        ],
        compiler_params=pltpu.CompilerParams(vmem_limit_bytes=4 << 20),
        name="placed",
    )(*results)


def solution(mesh):
    rows = P(("blk", "dp"), None)
    return jax.shard_map(
        shards,
        mesh=mesh,
        in_specs=(rows, rows, P(("blk", "dp")), P(), P(), P(), P()),
        out_specs=(rows, rows, P("blk", "dp")),
        check_vma=False,
    )
```

```python
import functools

import jax
import jax.numpy as jnp
from jax import lax
from jax.experimental import pallas as pl
from jax.experimental.pallas import tpu as pltpu
from jax.sharding import PartitionSpec as P

D = 1152
HEAD_COLS = 576
ROWS = 128
EPSILON = 1e-06
MESH = pl.DeviceIdType.MESH
NX, NY, NZ, NC, ZL = 4, 8, 12, 2, 4
GROUP = NX * NC
W_CHUNKS = 3
PLACE_PARTS = 2
IMG_PARTS = ((0, 64), (64, 32), (96, 32))
Y_ORDER = (4, 3, 5, 2, 6, 1, 7)
Z_ORDER = (6, 5, 7, 4, 8, 3, 9, 2, 10, 1, 11)
WC = D // W_CHUNKS


def device_at(x, y, z, c):
    x, y, z, c = lax.rem(x, NX), lax.rem(y, NY), lax.rem(z, NZ), lax.rem(c, NC)
    return ((z // ZL) * NY + y) * NC + c, x * ZL + lax.rem(z, ZL)


def coefficients(logits, ids, base):
    image_rows = base + lax.broadcasted_iota(jnp.int32, logits.shape, 0)
    match = image_rows == ids
    value = jax.nn.sigmoid(jnp.where(match, -logits, logits))
    return jnp.where(match, -value, value).astype(jnp.bfloat16)


def nt(left, right):
    return lax.dot_general(left, right, (((1,), (1,)), ((), ())), preferred_element_type=jnp.float32)


def tn(left, right):
    return lax.dot_general(left, right, (((0,), (0,)), ((), ())), preferred_element_type=jnp.float32)


def unit_scale(values):
    return lax.rsqrt(jnp.sum(values * values, axis=1, keepdims=True) + EPSILON)


def kernel(
    img_hbm, desc_hbm, ids_hbm, w_hbm, dw_hbm, scale_ref, bias_ref,
    image_out, text_out, head_ref,
    imgs, img_units, descs, ids, ids_prev, w, dw, pert, proj, text_unit,
    at_send, at_all, pt_send, pt_all, r_buf, y_own, y_send, y_recv, z_send, z_recv,
    local_sem, ring_send, ring_recv, a_send_sem, a_recv_sem, p_send_sem, p_recv_sem,
    y_send_sem, y_recv_sem, z_send_sem, z_recv_sem, word, ready, carried, help_recv, carry_send,
):
    b = lax.axis_index("blk")
    d = lax.axis_index("dp")
    c, y, z, x = lax.rem(b, 2), lax.rem(b // 2, NY), (b // (2 * NY)) * ZL + lax.rem(d, ZL), d // ZL
    after = (lax.rem(b + 1, 48), d)
    before = (lax.rem(b + 47, 48), d)
    group = [(i, f) for i in range(NX) for f in range(NC) if (i, f) != (0, 0)]

    loads = [
        pltpu.make_async_copy(desc_hbm, descs.at[pl.ds(0, ROWS)], local_sem.at[0]),
        pltpu.make_async_copy(img_hbm, imgs.at[pl.ds(0, ROWS)], local_sem.at[1]),
        pltpu.make_async_copy(ids_hbm, ids, local_sem.at[2]),
    ]
    loads[0].start()

    barrier = pltpu.get_barrier_semaphore()
    for i, f in group:
        pl.semaphore_signal(barrier, inc=1, device_id=device_at(x + i, y, z, c + f), device_id_type=MESH)
    across = (lax.rem(b + 47 + 2 * c, 48), d)
    goes_out = jnp.logical_and(y == 0, c == 0)
    comes_in = jnp.logical_and(y == NY - 1, c == 1)
    helps = jnp.logical_and(jnp.logical_or(y == NY - 1, y == 1), c == 0)
    helpers = [device_at(x, NY - 1, z + ZL, 0), device_at(x, 1, z + ZL, 0)]

    @pl.when(jnp.logical_not(goes_out))
    def _():
        pl.semaphore_signal(barrier, inc=1, device_id=across, device_id_type=MESH)

    @pl.when(comes_in)
    def _():
        for helper in helpers:
            pl.semaphore_signal(barrier, inc=1, device_id=helper, device_id_type=MESH)

    for j in (1, NY - 1):
        pl.semaphore_signal(barrier, inc=1, device_id=device_at(x, y + j, z, c), device_id_type=MESH)
    for j in (1, NZ - 1):
        pl.semaphore_signal(barrier, inc=1, device_id=device_at(x, y, z + j, c), device_id_type=MESH)

    for copy in loads[1:]:
        copy.start()
    w_loads = []
    for n in range(W_CHUNKS):
        cols = pl.ds(n * WC, WC)
        pair = [
            pltpu.make_async_copy(w_hbm.at[:, cols], w.at[:, cols], local_sem.at[3 + 2 * n]),
            pltpu.make_async_copy(dw_hbm.at[:, cols], dw.at[:, cols], local_sem.at[4 + 2 * n]),
        ]
        for copy in pair:
            copy.start()
        w_loads.append(pair)

    loads[0].wait()
    desc = descs[pl.ds(0, ROWS), :]
    turned = jnp.transpose(desc.astype(jnp.float32)).reshape(24, 2, 24, ROWS)
    for parity in range(2):
        at_send[parity] = turned[:, parity].reshape(HEAD_COLS, ROWS).astype(jnp.bfloat16)
    for copy in loads[1:]:
        copy.wait()

    pl.semaphore_wait(barrier, len(group) + 4 + jnp.where(comes_in, 0, 1) + jnp.where(helps, 1, 0))

    def pass_on(round_, along_y, along_z):
        for j in along_y:
            pl.semaphore_signal(
                word.at[2 * round_], inc=1, device_id=device_at(x, y + j, z, c), device_id_type=MESH
            )
        for j in along_z:
            pl.semaphore_signal(
                word.at[2 * round_ + 1], inc=1, device_id=device_at(x, y, z + j, c), device_id_type=MESH
            )


    def remote(src, dst, send, recv, device):
        return pltpu.make_async_remote_copy(
            src_ref=src, dst_ref=dst, send_sem=send, recv_sem=recv, device_id=device, device_id_type=MESH
        )

    def img_part(part, device):
        rows, n = IMG_PARTS[part]
        return remote(
            imgs.at[pl.ds(rows, n)], imgs.at[pl.ds(ROWS + rows, n)], ring_send.at[part], ring_recv.at[part], device
        )

    def help_part(part, device):
        rows, n = IMG_PARTS[part]
        return remote(imgs.at[pl.ds(rows, n)], carried, ring_send.at[part], help_recv, device)

    send_img = [img_part(part, before) for part in range(3)]

    @pl.when(goes_out)
    def _():
        pl.semaphore_signal(ready, inc=1, device_id=across, device_id_type=MESH)
        help_part(1, device_at(x, NY - 1, z, 0)).start()
        help_part(2, device_at(x, 1, z, 0)).start()
        send_img[0].start()

    def slot(i, core):
        return i * NC + core

    first = jnp.where(c == 0, NX - 1, 1)
    a_copies = []
    for n, (i, f) in enumerate([(first, 0), (first, 1), (0, 1), (NX - first, 0), (NX - first, 1)]):
        copy = remote(
            at_send.at[lax.rem(c + f, NC)], at_all.at[slot(i, c)],
            a_send_sem.at[n], a_recv_sem.at[slot(i, c)], device_at(x + i, y, z, c + f),
        )
        copy.start()
        a_copies.append(copy)

    @pl.when(jnp.logical_not(goes_out))
    def _():
        for copy in send_img:
            copy.start()

    def a_arrived(s):
        return remote(at_send.at[0], at_all.at[s], a_send_sem.at[0], a_recv_sem.at[s], before)

    def p_arrived(s):
        return remote(pt_send.at[0], pt_all.at[s], p_send_sem.at[0], p_recv_sem.at[s], before)

    pass_on(0, (1, NY - 1), (1, NZ - 1))

    for n in range(W_CHUNKS):
        cols = pl.ds(n * WC, WC)
        for copy in w_loads[n]:
            copy.wait()
        part = (w[:, cols].astype(jnp.float32) + dw[:, cols].astype(jnp.float32)).astype(jnp.bfloat16)
        pert[:, cols] = part
        proj[:, cols] = jnp.dot(descs[pl.ds(0, ROWS), :], part, preferred_element_type=jnp.float32)
    pl.semaphore_wait(word.at[0], 2)
    pl.semaphore_wait(word.at[1], 2)
    pass_on(1, (2, NY - 2), (2, NZ - 2))

    projected = proj[...]
    text_scale = unit_scale(projected)
    unit = projected * text_scale
    proj[...] = unit
    text_unit[pl.ds(0, ROWS), :] = unit.astype(jnp.bfloat16)

    img = imgs[pl.ds(0, ROWS), :].astype(jnp.float32)
    image_scale = unit_scale(img)
    img_units[pl.ds(0, ROWS), :] = (img * image_scale).astype(jnp.bfloat16)
    at_all[slot(0, c)] = at_send[c]

    carry = remote(
        carried,
        imgs.at[pl.ds(ROWS + IMG_PARTS[1][0] + jnp.where(y == 1, IMG_PARTS[1][1], 0), IMG_PARTS[1][1])],
        carry_send, ring_recv.at[jnp.where(y == 1, 2, 1)], device_at(x, NY - 1, z + NZ - ZL, 1),
    )

    @pl.when(helps)
    def _():
        help_part(1, before).wait_recv()
        carry.start()

    @pl.when(comes_in)
    def _():
        pl.semaphore_wait(ready, 1)

    send_desc = remote(descs.at[pl.ds(0, ROWS)], descs.at[pl.ds(ROWS, ROWS)], ring_send.at[3], ring_recv.at[3], after)
    send_ids = remote(ids, ids_prev, ring_send.at[4], ring_recv.at[4], after)
    send_desc.start()
    send_ids.start()

    handed = []
    for n, (i, core) in enumerate([(NX - 1, 0), (1, 1)]):
        a_arrived(slot(i, core)).wait_recv()
        copy = remote(
            at_all.at[slot(i, core)], at_all.at[slot(2, core)],
            a_send_sem.at[5 + n], a_recv_sem.at[slot(2, core)], device_at(x + i, y, z, c),
        )
        copy.start()
        handed.append(copy)

    scale = scale_ref[...]
    bias = bias_ref[...]
    row_base = (b * 16 + d) * ROWS
    next_base = (after[0] * 16 + d) * ROWS

    for copy in send_img:
        copy.wait_recv()
    img_next = imgs[pl.ds(ROWS, ROWS), :].astype(jnp.float32)
    img_units[pl.ds(ROWS, ROWS), :] = (img_next * unit_scale(img_next)).astype(jnp.bfloat16)
    logits = scale * nt(img_units[...], text_unit[pl.ds(0, ROWS), :]) + bias
    my_ids = ids[...]
    coef_own = coefficients(logits[:ROWS], my_ids, row_base)
    coef_next = coefficients(logits[ROWS:], my_ids, next_base)
    unit_text_grad = scale * tn(jnp.concatenate([coef_own, coef_next], axis=0), img_units[...])
    along = jnp.sum(unit * unit_text_grad, axis=1, keepdims=True)
    pre_grad = text_scale * (unit_text_grad - unit * along)
    pt = jnp.transpose(pre_grad[:, :HEAD_COLS])
    pt_send[...] = pt.reshape(NX, HEAD_COLS // NX, ROWS).astype(jnp.bfloat16)
    p_copies = []
    for n, (i, f) in enumerate([(2, 0), (2, 1), (1, 0), (1, 1), (3, 0), (3, 1), (0, 1)]):
        copy = remote(
            pt_send.at[lax.rem(x + i, NX)], pt_all.at[slot(i, c)],
            p_send_sem.at[n], p_recv_sem.at[slot(i, c)], device_at(x + i, y, z, c + f),
        )
        copy.start()
        p_copies.append(copy)
    pt_all[slot(0, c)] = pt_send[x]

    pl.semaphore_wait(word.at[2], 2)
    pl.semaphore_wait(word.at[3], 2)
    pass_on(2, (), (2, NZ - 2))

    text_out[...] = nt(pre_grad.astype(jnp.bfloat16), pert[...]).astype(jnp.bfloat16)

    def product(slots):
        features = jnp.concatenate([at_all[s] for s in slots], axis=1)
        columns = jnp.concatenate([pt_all[s] for s in slots], axis=1)
        return nt(features, columns)

    a_arrived(slot(0, 1 - c)).wait_recv()
    p_arrived(slot(0, 1 - c)).wait_recv()
    for i in (1, NX - 1):
        for core in range(NC):
            if (i, core) not in ((NX - 1, 0), (1, 1)):
                a_arrived(slot(i, core)).wait_recv()
            p_arrived(slot(i, core)).wait_recv()
    r_buf[:, pl.ds(0, 144)] = product([slot(i, core) for i in (0, 1, NX - 1) for core in range(NC)])
    for core in range(NC):
        a_arrived(slot(2, core)).wait_recv()
        p_arrived(slot(2, core)).wait_recv()
    r_buf[:, pl.ds(0, 144)] += product([slot(2, core) for core in range(NC)])
    low = r_buf[:, pl.ds(0, 128)].reshape(24, 3, 8, 128)
    high = r_buf[:, pl.ds(128, 128)].reshape(24, 3, 8, 128)
    lane = lax.broadcasted_iota(jnp.int32, (24, 8, 128), 2)

    def moved(values, shift):
        shift = shift % 128
        return pltpu.roll(values, shift, 2) if shift else values

    for k in range(ZL):
        parts = []
        for o in range(3):
            part = moved(low[:, o], 36 * o - 36 * k)
            if k == ZL - 1:
                part = jnp.where(lane < 36 * o + 20, part, moved(high[:, o], 36 * o + 20))
            parts.append(part)
        tile = jnp.where(lane < 36, parts[0], jnp.where(lane < 72, parts[1], parts[2]))
        tile = jnp.where(lane < 108, tile, 0.0).reshape(3, NY, 8, 128)
        for h in range(3):
            y_own[:, pl.ds((h * ZL + k) * 8, 8), :] = tile[h]
    y_send[...] = y_own[...].astype(jnp.bfloat16)
    y_copies = []
    for j in Y_ORDER:
        copy = remote(
            y_send.at[lax.rem(y + j, NY)], y_recv.at[j], y_send_sem.at[j], y_recv_sem.at[j], device_at(x, y + j, z, c)
        )
        copy.start()
        y_copies.append(copy)

    total = y_own[y]
    for j, copy in sorted(zip(Y_ORDER, y_copies), key=lambda e: min(e[0], NY - e[0])):
        copy.wait_recv()
        total = total + y_recv[j].astype(jnp.float32)
    pl.semaphore_wait(word.at[5], 2)
    z_send[...] = total.reshape(NZ, 8, 128)
    z_copies = []
    for j in Z_ORDER:
        copy = remote(
            z_send.at[lax.rem(z + j, NZ)], z_recv.at[j], z_send_sem.at[j], z_recv_sem.at[j], device_at(x, y, z + j, c)
        )
        copy.start()
        z_copies.append(copy)
    send_desc.wait_recv()
    send_ids.wait_recv()
    projected_prev = jnp.dot(descs[pl.ds(ROWS, ROWS), :], pert[...], preferred_element_type=jnp.float32)
    text_unit[pl.ds(ROWS, ROWS), :] = (projected_prev * unit_scale(projected_prev)).astype(jnp.bfloat16)
    logits_prev = scale * nt(img_units[pl.ds(0, ROWS), :], text_unit[pl.ds(ROWS, ROWS), :]) + bias
    coef_prev = coefficients(logits_prev, ids_prev[...], row_base)
    unit_image_grad = scale * jnp.dot(
        jnp.concatenate([coef_own, coef_prev], axis=1), text_unit[...], preferred_element_type=jnp.float32
    )
    img = imgs[pl.ds(0, ROWS), :].astype(jnp.float32)
    image_dir = img * image_scale
    along_image = jnp.sum(image_dir * unit_image_grad, axis=1, keepdims=True)
    image_out[...] = (image_scale * (unit_image_grad - image_dir * along_image)).astype(jnp.bfloat16)

    block = z_send[z]
    for j, copy in sorted(zip(Z_ORDER, z_copies), key=lambda e: min(e[0], NZ - e[0])):
        copy.wait_recv()
        block = block + z_recv[j]
    for o in range(3):
        head_ref[pl.ds(8 * o, 8), :] = (pltpu.roll(block, 128 - 36 * o, 1) if o else block)[:, :36]

    for copy in [*send_img, send_desc, send_ids, *a_copies, *handed, *p_copies, *y_copies, *z_copies]:
        copy.wait_send()

    @pl.when(helps)
    def _():
        carry.wait_send()


def placed(image_in, text_in, head_in, image_out, text_out, head_out, sem):
    copies = [pltpu.make_async_copy(head_in, head_out, sem.at[2 * PLACE_PARTS])]
    step = ROWS // PLACE_PARTS
    for n in range(PLACE_PARTS):
        rows = pl.ds(n * step, step)
        copies.append(pltpu.make_async_copy(image_in.at[rows], image_out.at[rows], sem.at[2 * n]))
        copies.append(pltpu.make_async_copy(text_in.at[rows], text_out.at[rows], sem.at[2 * n + 1]))
    for copy in copies:
        copy.start()
    for copy in copies:
        copy.wait()


def shards(img, desc, ids, w, dw, scale, bias):
    bf16, f32 = jnp.bfloat16, jnp.float32
    any_spec = pl.BlockSpec(memory_space=pl.ANY)
    dma = pltpu.SemaphoreType.DMA
    results = pl.pallas_call(
        kernel,
        out_shape=(
            pltpu.VMEM((ROWS, D), bf16),
            pltpu.VMEM((ROWS, D), bf16),
            pltpu.VMEM((24, 36), f32),
        ),
        in_specs=[any_spec] * 5 + [pl.BlockSpec(memory_space=pltpu.SMEM)] * 2,
        out_specs=(pl.BlockSpec(memory_space=pltpu.VMEM),) * 3,
        scratch_shapes=[
            pltpu.VMEM((2 * ROWS, D), bf16),
            pltpu.VMEM((2 * ROWS, D), bf16),
            pltpu.VMEM((2 * ROWS, D), bf16),
            pltpu.VMEM((1, ROWS), jnp.int32),
            pltpu.VMEM((1, ROWS), jnp.int32),
            pltpu.VMEM((D, D), bf16),
            pltpu.VMEM((D, D), bf16),
            pltpu.VMEM((D, D), bf16),
            pltpu.VMEM((ROWS, D), f32),
            pltpu.VMEM((2 * ROWS, D), bf16),
            pltpu.VMEM((2, HEAD_COLS, ROWS), bf16),
            pltpu.VMEM((GROUP, HEAD_COLS, ROWS), bf16),
            pltpu.VMEM((NX, HEAD_COLS // NX, ROWS), bf16),
            pltpu.VMEM((GROUP, HEAD_COLS // NX, ROWS), bf16),
            pltpu.VMEM((HEAD_COLS, 256), f32),
            pltpu.VMEM((NY, 96, 128), f32),
            pltpu.VMEM((NY, 96, 128), bf16),
            pltpu.VMEM((NY, 96, 128), bf16),
            pltpu.VMEM((NZ, 8, 128), f32),
            pltpu.VMEM((NZ, 8, 128), f32),
            dma((4 + 2 * W_CHUNKS,)),
            dma((5,)),
            dma((5,)),
            dma((GROUP,)),
            dma((GROUP,)),
            dma((GROUP,)),
            dma((GROUP,)),
            dma((NY,)),
            dma((NY,)),
            dma((NZ,)),
            dma((NZ,)),
            pltpu.SemaphoreType.REGULAR((6,)),
            pltpu.SemaphoreType.REGULAR,
            pltpu.VMEM((IMG_PARTS[1][1], D), bf16),
            dma,
            dma,
        ],
        compiler_params=pltpu.CompilerParams(
            collective_id=0, has_side_effects=True, vmem_limit_bytes=56 << 20
        ),
        name="contrastive",
    )(*(pltpu.with_memory_space_constraint(v, pltpu.HBM) for v in (img, desc, ids.reshape(1, ROWS), w, dw)), scale, bias)
    return pl.pallas_call(
        placed,
        out_shape=[jax.ShapeDtypeStruct(r.shape, r.dtype) for r in results],
        in_specs=[any_spec] * 3,
        out_specs=[any_spec] * 3,
        scratch_shapes=[
            dma((2 * PLACE_PARTS + 1,)),
        ],
        compiler_params=pltpu.CompilerParams(vmem_limit_bytes=4 << 20),
        name="placed",
    )(*results)


def solution(mesh):
    rows = P(("blk", "dp"), None)
    return jax.shard_map(
        shards,
        mesh=mesh,
        in_specs=(rows, rows, P(("blk", "dp")), P(), P(), P(), P()),
        out_specs=(rows, rows, P("blk", "dp")),
        check_vma=False,
    )
```
